256 devices in a mesh: blk: 16 (over x_hi, z), group: 16 (over x_lo, y, core).
Axes of the slice: x: 4 (x_hi: 2, x_lo: 2; x = x_hi * 2 + x_lo), y: 4, z: 8, core: 2. Of those that a mesh axis runs over, the one named last changes fastest.
Arguments:
- q_embed: bfloat16 [16, 2048, 1024], P('group', 'blk'), may hold values from -24 to 24
- t_embed: bfloat16 [16, 2048, 1024], P('group', 'blk'), may hold values from -24 to 24
- head: bfloat16 [1024, 1024], replicated, may hold values from -0.1875 to 0.1875
- positive: int32 [16, 2048], P('group', 'blk'), may hold values from 0 to 2047, each once within a row
- hard_ids: int32 [16, 2048, 4], P('group', 'blk'), may hold values from 0 to 32767, as said below
- loss_weight: float32 [16, 2048], P('group', 'blk'), may hold values from 1 to 8
Outputs:
- grad_q: bfloat16 [16, 2048, 1024], P('group', 'blk')
- grad_t: bfloat16 [16, 2048, 1024], P('group', 'blk')
- grad_head: float32 [1024, 1024], P(('blk', 'group'))
The draws below stay inside these ranges and needn't reach their ends.
Inputs may be any that keep to these rules, and one draw needn't show every extreme that they name: hard_ids[g, i, k] = g2 * 2048 + j names a table of another group g2 != g whose row j lies in the same block of 128 rows as i. Of the 512 slots (i, k) of one block of 128 rows, at most 70 name tables of any one group, and exactly 70 slots name tables of some group in every block; several slots may name the same table.
All inputs are finite; a program needn't handle non-finite values.
Results may differ from the reference program's by a relative error of at most 0.014.
Values may be sent and summed in bfloat16 or wider, within the bound.
A program may use at most 64 MiB of HBM per device.

```python
import math
import jax
import jax.numpy as jnp
from jax import lax

E = 1024
HARD = 4
TOK_DEV = 128
PAIRS = 2048
GROUPS = 16
CAP = 70


def table_rows(key):
    key = jax.random.fold_in(key, 17)
    first_key, second_key = jax.random.split(key)
    values = jax.random.normal(first_key, (GROUPS, PAIRS, E), jnp.float32) * 1.5
    row_scale = jnp.exp(jax.random.uniform(second_key, (GROUPS, PAIRS, 1), jnp.float32, math.log(0.6), math.log(1.8)))
    return values * row_scale


def hard_table_ids(key):
    key = jax.random.fold_in(key, 41)
    first_key, second_key, third_key = jax.random.split(key, 3)
    block_count = PAIRS // TOK_DEV
    device_count = GROUPS * block_count
    slot_count = HARD * TOK_DEV
    base_slots = jnp.broadcast_to(jnp.arange(slot_count, dtype=jnp.int32), (device_count, slot_count))
    shuffled = jax.random.permutation(first_key, base_slots, axis=1, independent=True)
    owner_rank = jnp.where(shuffled < CAP, 0, 1 + (shuffled - CAP) % (GROUPS - 2))
    base_owner = jnp.broadcast_to(jnp.arange(1, GROUPS, dtype=jnp.int32), (device_count, GROUPS - 1))
    owner_order = jax.random.permutation(second_key, base_owner, axis=1, independent=True)
    offsets = jnp.take_along_axis(owner_order, owner_rank, axis=1)
    device_ids = jnp.arange(device_count, dtype=jnp.int32)
    group_of = device_ids // block_count
    block_of = device_ids % block_count
    owner_group = (group_of[:, None] + offsets) % GROUPS
    row_pick = jax.random.randint(third_key, (device_count, slot_count), 0, TOK_DEV, jnp.int32)
    table_ids = owner_group * PAIRS + block_of[:, None] * TOK_DEV + row_pick
    return table_ids.reshape(GROUPS, PAIRS, HARD)


def draw_hard_ids(key, part):
    return hard_table_ids(key)


def draw_t_embed(key, part):
    values = table_rows(key)
    return jnp.clip(values, -24.0, 24.0).astype(jnp.bfloat16)


def draw_q_embed(key, part):
    values = table_rows(key)
    table_ids = hard_table_ids(key)
    key = jax.random.fold_in(key, 5)
    first_key = jax.random.fold_in(key, 0)
    flat_rows = values.reshape(GROUPS * PAIRS, E)
    hard_sum = flat_rows[table_ids[:, :, 0]]
    for column in range(1, HARD):
        hard_sum = hard_sum + flat_rows[table_ids[:, :, column]]
    result = jax.random.normal(first_key, (GROUPS, PAIRS, E), jnp.float32) * 1.5 + 0.12 * hard_sum
    return jnp.clip(result, -24.0, 24.0).astype(jnp.bfloat16)


def shard_levels(own_key, shape, cuts, low, high):
    gain, own = 1.0, jax.random.fold_in(own_key, 6)
    for dim, shards_of in cuts:
        steps = jnp.exp(jax.random.uniform(jax.random.fold_in(own, dim), (shards_of,), jnp.float32, low / len(cuts), high / len(cuts)))
        gain = gain * jnp.repeat(steps, shape[dim] // shards_of).reshape([-1 if axis == dim else 1 for axis in range(len(shape))])
    return gain


def normal_values(key, dims, deviation, reach, kind=jnp.bfloat16):
    return jnp.clip(deviation * jax.random.normal(key, dims, jnp.float32), -reach, reach).astype(kind)


def setup_inputs(seed: int = 0) -> dict:
    keys = jax.random.split(jax.random.key(seed), 7)
    return {
        "q_embed": draw_q_embed(jax.random.fold_in(keys[6], 71), 0),
        "t_embed": draw_t_embed(jax.random.fold_in(keys[6], 71), 0),
        "head": normal_values(keys[2], (E, E), E ** -0.5, 0.1875),
        "positive": jax.vmap(lambda own: jax.random.permutation(own, PAIRS))(jax.random.split(keys[3], GROUPS)).reshape((GROUPS, PAIRS)).astype(jnp.int32),
        "hard_ids": draw_hard_ids(jax.random.fold_in(keys[6], 71), 0),
        "loss_weight": jnp.clip(jnp.exp(math.log(8.0) - 2.0794415 * jax.random.uniform(keys[5], (GROUPS, PAIRS), jnp.float32) ** shard_levels(keys[5], (GROUPS, PAIRS), ((0, 16), (1, 16)), -0.2, 0.2)), 1.0, 8.0),
    }


def reference(q_embed, t_embed, head, positive, hard_ids, loss_weight):
    group_count, pair_count, feat_width = q_embed.shape
    logit_scale = feat_width ** -0.5
    queries = jnp.dot(q_embed.reshape(-1, feat_width), head, preferred_element_type=jnp.float32).astype(jnp.bfloat16)
    table_keys = jnp.dot(t_embed.reshape(-1, feat_width), head, preferred_element_type=jnp.float32).astype(jnp.bfloat16)
    flat_keys = table_keys
    queries = queries.reshape(group_count, pair_count, feat_width)
    group_keys_all = table_keys.reshape(group_count, pair_count, feat_width)
    columns = jnp.arange(pair_count, dtype=jnp.int32)

    def one_group(carry, inputs):
        group_q, group_t, target_row, wanted, weight_row = inputs
        negatives = flat_keys[wanted]
        scores = logit_scale * jnp.dot(group_q, group_t.T, preferred_element_type=jnp.float32)
        hard_scores = logit_scale * jnp.einsum('pe,pke->pk', group_q.astype(jnp.float32), negatives.astype(jnp.float32))
        row_max = jnp.maximum(jnp.max(scores, axis=1), jnp.max(hard_scores, axis=1))
        row_total = jnp.sum(jnp.exp(scores - row_max[:, None]), axis=1) + jnp.sum(jnp.exp(hard_scores - row_max[:, None]), axis=1)
        log_total = row_max + jnp.log(row_total)
        is_target = (target_row[:, None] == columns[None, :]).astype(jnp.float32)
        score_grad = (weight_row[:, None] * (jnp.exp(scores - log_total[:, None]) - is_target)).astype(jnp.bfloat16)
        hard_grad = (weight_row[:, None] * jnp.exp(hard_scores - log_total[:, None])).astype(jnp.bfloat16)
        query_grad = logit_scale * (jnp.dot(score_grad, group_t, preferred_element_type=jnp.float32)
                                    + jnp.einsum('pk,pke->pe', hard_grad.astype(jnp.float32), negatives.astype(jnp.float32)))
        table_in = logit_scale * jnp.dot(score_grad.T, group_q, preferred_element_type=jnp.float32)
        hard_rows = (logit_scale * hard_grad.astype(jnp.float32)[:, :, None] * group_q.astype(jnp.float32)[:, None, :]).astype(jnp.bfloat16)
        carry = carry.at[wanted.reshape(-1)].add(hard_rows.reshape(-1, feat_width).astype(jnp.float32))
        return carry, (query_grad.astype(jnp.bfloat16), table_in)

    start_sum = jnp.zeros((group_count * pair_count, feat_width), jnp.float32)
    table_hard, (query_grad, table_in) = lax.scan(one_group, start_sum, (queries, group_keys_all, positive, hard_ids, loss_weight))
    table_grad = (table_in + table_hard.reshape(group_count, pair_count, feat_width)).astype(jnp.bfloat16)
    flat_qgrad = query_grad.reshape(-1, feat_width)
    flat_tgrad = table_grad.reshape(-1, feat_width)
    grad_q = jnp.dot(flat_qgrad, head.T, preferred_element_type=jnp.float32).astype(jnp.bfloat16)
    grad_t = jnp.dot(flat_tgrad, head.T, preferred_element_type=jnp.float32).astype(jnp.bfloat16)
    grad_head = (jnp.dot(q_embed.reshape(-1, feat_width).T, flat_qgrad, preferred_element_type=jnp.float32)
                 + jnp.dot(t_embed.reshape(-1, feat_width).T, flat_tgrad, preferred_element_type=jnp.float32))
    return (grad_q.reshape(group_count, pair_count, feat_width),
            grad_t.reshape(group_count, pair_count, feat_width),
            grad_head)
```

```python
import functools
import math

import jax
import jax.numpy as jnp
from jax import lax
from jax.experimental import pallas as pl
from jax.experimental.pallas import tpu as pltpu
from jax.sharding import PartitionSpec as P

MESH = pl.DeviceIdType.MESH
F32 = jnp.float32
BF16 = jnp.bfloat16

NZ = 8
NY = 4
NEG = -1e30


Z_AG, Y_AG, C_AG, X_IN, STAT = 0, 8, 12, 16, 20
Z_RS, C_RS, Y_RS, X_OUT = 23, 31, 35, 39
H_C, H_Y, H_X, H_Z, H_C2 = 41, 42, 45, 48, 55
COPIES = 56


def nn(left, right):
    return lax.dot_general(left, right, (((1,), (0,)), ((), ())), preferred_element_type=F32)


def nt(left, right):
    return lax.dot_general(left, right, (((1,), (1,)), ((), ())), preferred_element_type=F32)


def tn(left, right):
    return lax.dot_general(left, right, (((0,), (0,)), ((), ())), preferred_element_type=F32)


def span(i, size):
    return pl.ds(pl.multiple_of(i * size, size), size)


def loop(count, unroll=1):
    def run(step):
        lax.fori_loop(0, count, lambda i, carry: (step(i), carry)[1], 0, unroll=unroll)
    return run


def kernel(
    qe_ref, te_ref, head_ref, meta_ref, gq_ref, gt_ref, gh_ref,
    xa, qq, qp, tz, ty, meta, s_in, s_hd, g_in, g_hd, st_in, st_hd, stat, lse,
    zs, zr, zown, cs, cr, yown, ys, yr, acc, qgs, qgr,
    h2, hcs, hcr, hys, hyr, hxs, hxr, hzs, hzr, hc2s, hc2r,
    send_sem, recv_sem,
):
    rows, feat = qe_ref.shape
    half = rows // 2
    scale = feat ** -0.5
    cols = NZ * rows
    fhalf = feat // 2
    blk, grp = lax.axis_index("blk"), lax.axis_index("group")
    xh, z = lax.div(blk, NZ), lax.rem(blk, NZ)
    xl, y, c = lax.div(grp, 2 * NY), lax.rem(lax.div(grp, 2), NY), lax.rem(grp, 2)

    def at(dz=0, dy=0, dx=0, dc=0):
        xh2 = 1 - xh if dx & 2 else xh
        xl2 = 1 - xl if dx & 1 else xl
        c2 = 1 - c if dc else c
        z2, y2 = lax.rem(z + dz + NZ, NZ), lax.rem(y + dy + NY, NY)
        return (xh2 * NZ + z2, (xl2 * NY + y2) * 2 + c2)

    def copy(src, dst, sem, device):
        return pltpu.make_async_remote_copy(
            src_ref=src, dst_ref=dst, send_sem=send_sem.at[sem], recv_sem=recv_sem.at[sem],
            device_id=device, device_id_type=MESH,
        )

    peers = (
        [at(dz=d) for d in range(1, NZ)] + [at(dy=d) for d in range(1, NY)]
        + [at(dx=d) for d in (1, 2, 3)] + [at(dc=1)]
    )
    barrier = pltpu.get_barrier_semaphore()
    for peer in peers:
        pl.semaphore_signal(barrier, inc=1, device_id=peer, device_id_type=MESH)
    pl.semaphore_wait(barrier, len(peers))

    started = []

    def start(*args):
        one = copy(*args)
        one.start()
        started.append(one)
        return one

    zright, zleft = at(dz=1), at(dz=-1)
    yright, yleft = at(dy=1), at(dy=-1)
    core = at(dc=1)
    lo, hi = pl.ds(0, half), pl.ds(half, half)

    zag_r, zag_l = {}, {}
    zag_r[1] = start(te_ref, tz.at[NZ - 1], Z_AG + 0, zright)
    zag_l[1] = start(te_ref, tz.at[1], Z_AG + 1, zleft)
    x1 = start(qe_ref, xa.at[pl.ds(0, rows)], X_IN + 0, at(dx=1))
    x2 = start(qe_ref, xa.at[pl.ds(2 * rows, rows)], X_IN + 1, at(dx=2))
    yag_r = start(te_ref, ty.at[3], Y_AG + 0, yright)
    yag_l = start(te_ref, ty.at[1], Y_AG + 1, yleft)
    cag = [start(te_ref, ty.at[4], C_AG + 0, core)]
    m1 = start(meta_ref, meta.at[pl.ds(0, rows)], X_IN + 2, at(dx=1))
    m2 = start(meta_ref, meta.at[pl.ds(2 * rows, rows)], X_IN + 3, at(dx=2))

    tz[0] = te_ref[...]
    ty[0] = te_ref[...]
    xa[pl.ds(rows, rows), :] = qe_ref[...]
    meta[pl.ds(rows, rows), :] = meta_ref[...]

    def project(first, count):
        own = pl.ds(first, count)

        def forward(i):
            part = nn(xa[own, :], head_ref[:, span(i, 256)]).astype(BF16)
            qq[lax.div(i, 2), pl.ds(3 * rows + first, count), span(lax.rem(i, 2), 256)] = part

        loop(feat // 256)(forward)

        def back(i):
            block = span(i, 256)
            total = nt(qq[0, pl.ds(3 * rows + first, count), :], head_ref[block, pl.ds(0, fhalf)])
            total += nt(qq[1, pl.ds(3 * rows + first, count), :], head_ref[block, pl.ds(fhalf, fhalf)])
            qp[own, block] = (scale * total).astype(BF16)

        loop(feat // 256)(back)

    def z_pass(step):
        zag_r[step].wait_recv()
        zag_l[step].wait_recv()
        if step < 3:
            zag_r[step + 1] = start(tz.at[NZ - step], tz.at[NZ - step - 1], Z_AG + 2 * step, zright)
            zag_l[step + 1] = start(tz.at[step], tz.at[step + 1], Z_AG + 2 * step + 1, zleft)
        elif step == 3:
            zag_r[4] = start(tz.at[5, lo], tz.at[4, lo], Z_AG + 6, zright)
            zag_l[4] = start(tz.at[3, hi], tz.at[4, hi], Z_AG + 7, zleft)

    def score_in(slot):
        s_in[:, pl.ds(slot * rows, rows)] = nt(qp[pl.ds(rows, 2 * rows), :], tz[slot])

    project(rows, rows)
    z_pass(1)
    yag_r.wait_recv()
    yag_l.wait_recv()
    yag2_r = start(ty.at[3, lo], ty.at[2, lo], Y_AG + 2, yright)
    yag2_l = start(ty.at[1, hi], ty.at[2, hi], Y_AG + 3, yleft)
    cag.append(start(ty.at[3], ty.at[7], C_AG + 1, core))
    cag.append(start(ty.at[1], ty.at[5], C_AG + 2, core))
    x1.wait_recv()
    x2.wait_recv()
    m1.wait_recv()
    m2.wait_recv()
    project(0, rows)
    project(2 * rows, rows)
    z_pass(2)
    for slot in (0, 1, 7):
        score_in(slot)
    yag2_r.wait_recv()
    yag2_l.wait_recv()
    cag.append(start(ty.at[2], ty.at[6], C_AG + 3, core))
    for one in cag:
        one.wait_recv()

    def score_hard(i):
        s_hd[:, span(i, rows)] = nt(qp[pl.ds(0, 2 * rows), :], ty[i])

    loop(2 * NY)(score_hard)

    lane = lax.broadcasted_iota(jnp.int32, (1, cols), 1)
    slot_of, row_of = lane // rows, lane % rows
    other = slot_of // NY
    owner_core = c + other - 2 * c * other
    owner = (xl * NY + lax.rem(y + slot_of % NY, NY)) * 2 + owner_core
    pairs = 2 * cols
    hard_col = (owner * pairs + blk * rows + row_of).astype(F32)
    in_col = (xh * cols + lax.rem(z * rows + lane, cols)).astype(F32)

    def stats_of(scores, out, block):
        top = jnp.max(scores, axis=1, keepdims=True)
        total = jnp.sum(jnp.exp(scores - top), axis=1, keepdims=True)
        place = lax.broadcasted_iota(jnp.int32, (scores.shape[0], 128), 1)
        out[block, :] = jnp.where(place == 0, top, total)

    def mask_hard(i):
        block = span(i, 32)
        named = meta[block, :]
        count = jnp.zeros((32, cols), F32)
        for k in range(4):
            count += jnp.where(named[:, 2 + k:3 + k] == hard_col, 1.0, 0.0)
        kept = jnp.where(count > 0.0, s_hd[block, :] + jnp.log(jnp.maximum(count, 1.0)), NEG)
        s_hd[block, :] = kept
        stats_of(kept, st_hd, block)

    z_pass(3)
    loop(2 * rows // 32)(mask_hard)
    for slot in (2, 6, 3, 5):
        score_in(slot)
    z_pass(4)
    score_in(4)

    def stats_in(i):
        block = span(i, 32)
        stats_of(s_in[block, :], st_in, block)

    loop(2 * rows // 32)(stats_in)

    a0, b0 = st_in[pl.ds(0, rows), 0:1], st_in[pl.ds(0, rows), 1:2]
    a1, b1 = st_hd[pl.ds(rows, rows), 0:1], st_hd[pl.ds(rows, rows), 1:2]
    top = jnp.maximum(a0, a1)
    total = b0 * jnp.exp(a0 - top) + b1 * jnp.exp(a1 - top)
    place = lax.broadcasted_iota(jnp.int32, (rows, 128), 1)
    packed = jnp.zeros((rows, 128), F32)
    for where, value in enumerate((
        top, total,
        st_in[pl.ds(rows, rows), 0:1], st_in[pl.ds(rows, rows), 1:2],
        st_hd[pl.ds(0, rows), 0:1], st_hd[pl.ds(0, rows), 1:2],
    )):
        packed = jnp.where(place == where, value, packed)
    stat[0] = packed
    shared = [start(stat.at[0], stat.at[d], STAT + d - 1, at(dx=d)) for d in (1, 2, 3)]
    for one in shared:
        one.wait_recv()

    def combine(parts):
        tops = [stat[d, :, w:w + 1] for d, w in parts]
        totals = [stat[d, :, w + 1:w + 2] for d, w in parts]
        top = functools.reduce(jnp.maximum, tops)
        total = sum(t * jnp.exp(m - top) for m, t in zip(tops, totals))
        return jnp.broadcast_to(top + jnp.log(total), (rows, 128))

    lse[pl.ds(0, rows), :] = combine([(0, 4), (1, 0), (3, 2)])
    lse[pl.ds(rows, rows), :] = combine([(0, 0), (1, 4), (2, 2)])
    lse[pl.ds(2 * rows, rows), :] = combine([(0, 2), (2, 0), (3, 4)])

    def grad_in(i):
        block = span(i, 32)
        wide = pl.ds(pl.multiple_of(rows + i * 32, 32), 32)
        info = meta[wide, :]
        prob = jnp.exp(s_in[block, :] - lse[wide, 0:1])
        hot = jnp.where(info[:, 1:2] == in_col, 1.0, 0.0)
        g_in[block, :] = (info[:, 0:1] * (prob - hot)).astype(BF16)

    loop(2 * rows // 32)(grad_in)

    def table_in(slot):
        return tn(g_in[:, pl.ds(slot * rows, rows)], qp[pl.ds(rows, 2 * rows), :])

    first = table_in(4).astype(BF16)
    zs[0, lo] = first[:half]
    zs[1, hi] = first[half:]
    zrs_r, zrs_l = {}, {}
    zrs_r[1] = start(zs.at[0, lo], zr.at[0, lo], Z_RS + 0, zright)
    zrs_l[1] = start(zs.at[1, hi], zr.at[1, hi], Z_RS + 1, zleft)

    def z_sum(step):
        zrs_r[step].wait_recv()
        zrs_l[step].wait_recv()
        i, j = 2 * (step - 1), 2 * step
        if step == 1:
            zs[j, lo] = (zown[0, lo] + zr[i, lo].astype(F32)).astype(BF16)
            zs[j, hi] = zown[0, hi].astype(BF16)
            zs[j + 1, lo] = zown[1, lo].astype(BF16)
            zs[j + 1, hi] = (zown[1, hi] + zr[i + 1, hi].astype(F32)).astype(BF16)
        else:
            zs[j] = (zown[2 * step - 2] + zr[i].astype(F32)).astype(BF16)
            zs[j + 1] = (zown[2 * step - 1] + zr[i + 1].astype(F32)).astype(BF16)
        zrs_r[step + 1] = start(zs.at[j], zr.at[j], Z_RS + j, zright)
        zrs_l[step + 1] = start(zs.at[j + 1], zr.at[j + 1], Z_RS + j + 1, zleft)

    zown[0] = table_in(3)
    zown[1] = table_in(5)

    def grad_hard(i):
        block = span(i, 32)
        prob = jnp.exp(s_hd[block, :] - lse[block, 0:1])
        g_hd[block, :] = (meta[block, 0:1] * prob).astype(BF16)

    loop(2 * rows // 32)(grad_hard)

    def table_hard(i):
        return tn(g_hd[:, span(i, rows)], qp[pl.ds(0, 2 * rows), :])

    def cross(i):
        cs[i] = table_hard(NY + i).astype(BF16)

    z_sum(1)

    def ahead(i):
        block = span(i, 256)
        a_in, a_hd = jnp.zeros((2 * rows, 256), F32), jnp.zeros((2 * rows, 256), F32)
        for slot in range(NZ):
            part = pl.ds(slot * rows, rows)
            a_in += nn(g_in[:, part], tz[slot, :, block])
            a_hd += nn(g_hd[:, part], ty[slot, :, block])
        at0 = 3 * rows
        xa[pl.ds(at0, rows), block] = (scale * a_hd[:rows]).astype(BF16)
        xa[pl.ds(at0 + rows, rows), block] = (scale * (a_hd[rows:] + a_in[:rows])).astype(BF16)
        xa[pl.ds(at0 + 2 * rows, rows), block] = (scale * a_in[rows:]).astype(BF16)

    loop(feat // 256)(ahead)

    def through(i):
        part = nn(xa[pl.ds(3 * rows, 3 * rows), :], head_ref[:, span(i, 256)])
        qq[lax.div(i, 2), pl.ds(0, 3 * rows), span(lax.rem(i, 2), 256)] = part.astype(BF16)
        acc[:, span(i, 256)] = part[rows:2 * rows]
        qgs[0, :, span(i, 256)] = part[:rows].astype(BF16)
        qgs[1, :, span(i, 256)] = part[2 * rows:].astype(BF16)

    loop(feat // 256)(through)
    back1 = start(qgs.at[0], qgr.at[0], X_OUT + 0, at(dx=1))
    back2 = start(qgs.at[1], qgr.at[1], X_OUT + 1, at(dx=2))

    def head_part(which):
        def one(i):
            block = span(i, 256)
            h2[which, block, :] = tn(xa[:, block], qq[which])
        loop(feat // 256)(one)

    head_part(1 - c)
    hcs[...] = h2[1 - c].astype(BF16)
    hc = start(hcs, hcr, H_C, core)
    zown[2] = table_in(2)
    zown[3] = table_in(6)
    z_sum(2)
    loop(NY)(cross)
    crs = [start(cs.at[i], cr.at[i], C_RS + i, core) for i in range(NY)]
    head_part(c)

    groups = feat // (8 * NY)
    hc.wait_recv()

    def join(i):
        block = span(i, 128)
        h2[c, block, :] = h2[c, block, :] + hcr[block, :].astype(F32)

    loop(feat // 128)(join)
    view_y = h2.at[c].reshape(groups, NY, 8, fhalf)
    hy = []
    for d in (1, 2, 3):
        there = lax.rem(y + d, NY)
        hys[d - 1] = view_y[:, there].reshape(groups * 8, fhalf).astype(BF16)
        hy.append(start(hys.at[d - 1], hyr.at[d - 1], H_Y + d - 1, at(dy=d)))

    for one in crs:
        one.wait_recv()

    def own_hard(i):
        yown[i] = table_hard(i) + cr[i].astype(F32)

    loop(NY)(own_hard)
    ys[0, lo] = yown[2, lo].astype(BF16)
    ys[1, hi] = yown[2, hi].astype(BF16)
    yrs_r = start(ys.at[0, lo], yr.at[0, lo], Y_RS + 0, yright)
    yrs_l = start(ys.at[1, hi], yr.at[1, hi], Y_RS + 1, yleft)
    zown[4] = table_in(1)
    zown[5] = table_in(7)
    z_sum(3)
    zown[6] = table_in(0)

    for one in hy:
        one.wait_recv()
    mine = view_y[:, y].reshape(groups * 8, fhalf)
    for d in range(3):
        mine = mine + hyr[d].astype(F32)
    h2[0, pl.ds(0, groups * 8), :] = mine
    view_x = h2.at[0, pl.ds(0, groups * 8)].reshape(2, NZ, 2, 8, fhalf)
    hx = []
    for d in (1, 2, 3):
        xh2 = 1 - xh if d & 2 else xh
        xl2 = 1 - xl if d & 1 else xl
        hxs[d - 1] = view_x[xh2, :, xl2].reshape(NZ * 8, fhalf).astype(BF16)
        hx.append(start(hxs.at[d - 1], hxr.at[d - 1], H_X + d - 1, at(dx=d)))

    yrs_r.wait_recv()
    yrs_l.wait_recv()
    ys[2, lo] = (yown[1, lo] + yr[0, lo].astype(F32)).astype(BF16)
    ys[2, hi] = yown[1, hi].astype(BF16)
    ys[3, lo] = yown[3, lo].astype(BF16)
    ys[3, hi] = (yown[3, hi] + yr[1, hi].astype(F32)).astype(BF16)
    yrs2_r = start(ys.at[2], yr.at[2], Y_RS + 2, yright)
    yrs2_l = start(ys.at[3], yr.at[3], Y_RS + 3, yleft)

    for one in hx:
        one.wait_recv()
    small = view_x[xh, :, xl].reshape(NZ * 8, fhalf)
    for d in range(3):
        small = small + hxr[d].astype(F32)
    hzs[...] = small.reshape(NZ, 8, fhalf)
    hz = [
        start(hzs.at[lax.rem(z + d, NZ)], hzr.at[d - 1], H_Z + d - 1, at(dz=d))
        for d in range(1, NZ)
    ]

    back1.wait_recv()
    back2.wait_recv()
    query_grad = (acc[...] + qgr[0].astype(F32) + qgr[1].astype(F32)).astype(BF16)
    qgs_own = query_grad

    def question(i):
        block = span(i, 256)
        gq_ref[:, block] = nt(qgs_own, head_ref[block, :]).astype(BF16)

    loop(feat // 256)(question)

    for one in hz:
        one.wait_recv()
    last = hzs[z]
    for d in range(NZ - 1):
        last = last + hzr[d]
    hc2s[...] = last
    hc2 = start(hc2s, hc2r, H_C2, core)

    yrs2_r.wait_recv()
    yrs2_l.wait_recv()
    zown[6] = zown[6] + yown[0] + yr[2].astype(F32) + yr[3].astype(F32)
    zrs_r[4].wait_recv()
    zrs_l[4].wait_recv()
    gt_ref[...] = (zown[6] + zr[6].astype(F32) + zr[7].astype(F32)).astype(BF16)

    hc2.wait_recv()
    theirs = hc2r[...]
    picked_own = jnp.where(c == 0, last[0:4], last[4:8])
    picked = jnp.where(c == 0, theirs[0:4], theirs[4:8])
    gh_ref[:, pl.ds(0, fhalf)] = jnp.where(c == 0, picked_own, picked)
    gh_ref[:, pl.ds(fhalf, fhalf)] = jnp.where(c == 0, picked, picked_own)

    for one in started:
        one.wait_send()


def body(q_embed, t_embed, head, positive, hard_ids, loss_weight):
    rows, feat = q_embed.shape[1:]
    cols, fhalf = NZ * rows, feat // 2
    meta = jnp.concatenate(
        [
            loss_weight[0][:, None],
            positive[0][:, None].astype(F32),
            hard_ids[0].astype(F32),
            jnp.zeros((rows, 122), F32),
        ],
        axis=1,
    )
    vmem = pl.BlockSpec(memory_space=pltpu.VMEM)
    shapes = [
        ((6 * rows, feat), BF16),
        ((2, 6 * rows, fhalf), BF16),
        ((3 * rows, feat), BF16),
        ((NZ, rows, feat), BF16),
        ((2 * NY, rows, feat), BF16),
        ((3 * rows, 128), F32),
        ((2 * rows, cols), F32),
        ((2 * rows, cols), F32),
        ((2 * rows, cols), BF16),
        ((2 * rows, cols), BF16),
        ((2 * rows, 128), F32),
        ((2 * rows, 128), F32),
        ((4, rows, 128), F32),
        ((3 * rows, 128), F32),
        ((8, rows, feat), BF16),
        ((8, rows, feat), BF16),
        ((7, rows, feat), F32),
        ((NY, rows, feat), BF16),
        ((NY, rows, feat), BF16),
        ((NY, rows, feat), F32),
        ((4, rows, feat), BF16),
        ((4, rows, feat), BF16),
        ((rows, feat), F32),
        ((2, rows, feat), BF16),
        ((2, rows, feat), BF16),
        ((2, feat, fhalf), F32),
        ((feat, fhalf), BF16),
        ((feat, fhalf), BF16),
        ((3, feat // NY, fhalf), BF16),
        ((3, feat // NY, fhalf), BF16),
        ((3, NZ * 8, fhalf), BF16),
        ((3, NZ * 8, fhalf), BF16),
        ((NZ, 8, fhalf), F32),
        ((NZ - 1, 8, fhalf), F32),
        ((8, fhalf), F32),
        ((8, fhalf), F32),
    ]
    grad_q, grad_t, grad_head = pl.pallas_call(
        kernel,
        out_shape=(
            jax.ShapeDtypeStruct((rows, feat), BF16),
            jax.ShapeDtypeStruct((rows, feat), BF16),
            jax.ShapeDtypeStruct((4, feat), F32),
        ),
        in_specs=[vmem] * 4,
        out_specs=(vmem, vmem, vmem),
        scratch_shapes=[pltpu.VMEM(s, t) for s, t in shapes] + [
            pltpu.SemaphoreType.DMA((COPIES,)),
            pltpu.SemaphoreType.DMA((COPIES,)),
        ],
        compiler_params=pltpu.CompilerParams(
            collective_id=0, has_side_effects=True, vmem_limit_bytes=56 * 1024 * 1024
        ),
    )(q_embed[0], t_embed[0], head, meta)
    return (grad_q[None], grad_t[None], grad_head)


def solution(mesh):
    in_specs = (
        P("group", "blk", None),
        P("group", "blk", None),
        P(),
        P("group", "blk"),
        P("group", "blk", None),
        P("group", "blk"),
    )
    out_specs = (P("group", "blk", None), P("group", "blk", None), P(("blk", "group"), None))
    return jax.shard_map(body, mesh=mesh, in_specs=in_specs, out_specs=out_specs, check_vma=False)
```

```python
import functools
import math

import jax
import jax.numpy as jnp
from jax import lax
from jax.experimental import pallas as pl
from jax.experimental.pallas import tpu as pltpu
from jax.sharding import PartitionSpec as P

MESH = pl.DeviceIdType.MESH
F32 = jnp.float32
BF16 = jnp.bfloat16

NZ = 8
NY = 4
NEG = -1e30


Z_AG, Y_AG, C_AG, X_IN, STAT = 0, 14, 18, 22, 26
Z_RS, C_RS, Y_RS, X_OUT = 29, 43, 47, 51
H_C, H_A1, H_B1, H_A2, H_B2, H_Z, H_C2 = 53, 54, 57, 60, 63, 66, 73
COPIES = 74


def nn(left, right):
    return lax.dot_general(left, right, (((1,), (0,)), ((), ())), preferred_element_type=F32)


def nt(left, right):
    return lax.dot_general(left, right, (((1,), (1,)), ((), ())), preferred_element_type=F32)


def tn(left, right):
    return lax.dot_general(left, right, (((0,), (0,)), ((), ())), preferred_element_type=F32)


def span(i, size):
    return pl.ds(pl.multiple_of(i * size, size), size)


def loop(count, unroll=1):
    def run(step):
        lax.fori_loop(0, count, lambda i, carry: (step(i), carry)[1], 0, unroll=unroll)
    return run


def kernel(
    qe_ref, te_ref, head_ref, weight_ref, positive_ref, ids_ref, gq_ref, gt_ref, gh_ref,
    xa, qq, qp, tz, ty, meta, info, s_in, s_hd, g_in, g_hd, st_in, st_hd, stat, wide, alpha,
    zs, zr, zown, cs, cr, yown, ys, yr, acc, qgs, qgr,
    h2, hcs, hcr, h1s, h1r, hm, h2s, h2r, hzs, hzr, hc2s, hc2r,
    send_sem, recv_sem,
):
    rows, feat = qe_ref.shape
    half = rows // 2
    scale = feat ** -0.5
    cols = NZ * rows
    fhalf, fq = feat // 2, feat // 4
    blk, grp = lax.axis_index("blk"), lax.axis_index("group")
    xh, z = lax.div(blk, NZ), lax.rem(blk, NZ)
    xl, y, c = lax.div(grp, 2 * NY), lax.rem(lax.div(grp, 2), NY), lax.rem(grp, 2)

    def at(dz=0, dy=0, dx=0, dc=0):
        xh2 = 1 - xh if dx & 2 else xh
        xl2 = 1 - xl if dx & 1 else xl
        c2 = 1 - c if dc else c
        z2, y2 = lax.rem(z + dz + NZ, NZ), lax.rem(y + dy + NY, NY)
        return (xh2 * NZ + z2, (xl2 * NY + y2) * 2 + c2)

    def copy(src, dst, sem, device):
        return pltpu.make_async_remote_copy(
            src_ref=src, dst_ref=dst, send_sem=send_sem.at[sem], recv_sem=recv_sem.at[sem],
            device_id=device, device_id_type=MESH,
        )

    peers = (
        [at(dz=d) for d in range(1, NZ)] + [at(dy=d) for d in range(1, NY)]
        + [at(dx=d) for d in (1, 2, 3)] + [at(dc=1)]
    )
    barrier = pltpu.get_barrier_semaphore()
    for peer in peers:
        pl.semaphore_signal(barrier, inc=1, device_id=peer, device_id_type=MESH)

    meta[1, 0:1, :] = weight_ref[...]
    meta[1, 1:2, :] = positive_ref[...].astype(F32)
    meta[1, 2:6, :] = ids_ref[...].astype(F32)
    meta[1, 6:8, :] = jnp.zeros((2, rows), F32)
    pl.semaphore_wait(barrier, len(peers))

    started = []

    def start(*args):
        one = copy(*args)
        one.start()
        started.append(one)
        return one

    zright, zleft = at(dz=1), at(dz=-1)
    yright, yleft = at(dy=1), at(dy=-1)
    core = at(dc=1)
    lo, hi = pl.ds(0, half), pl.ds(half, half)

    za, zb = {}, {}

    def gather_a(k):
        src = (te_ref.at[lo], te_ref.at[hi]) if k == 0 else (tz.at[NZ - k, lo], tz.at[k, hi])
        za[k] = (
            start(src[0], tz.at[NZ - 1 - k, lo], Z_AG + 2 * k, zright),
            start(src[1], tz.at[1 + k, hi], Z_AG + 2 * k + 1, zleft),
        )

    def gather_b(k):
        src = (te_ref.at[hi], te_ref.at[lo]) if k == 0 else (tz.at[NZ - k, hi], tz.at[k, lo])
        zb[k] = (
            start(src[0], tz.at[NZ - 1 - k, hi], Z_AG + 8 + 2 * k, zright),
            start(src[1], tz.at[1 + k, lo], Z_AG + 9 + 2 * k, zleft),
        )

    def arrive(pair):
        pair[0].wait_recv()
        pair[1].wait_recv()

    gather_a(0)
    m2 = start(meta.at[1], meta.at[2], X_IN + 3, at(dx=2))
    m1 = start(meta.at[1], meta.at[0], X_IN + 2, at(dx=1))
    x2 = start(qe_ref, xa.at[pl.ds(2 * rows, rows)], X_IN + 1, at(dx=2))
    x1 = start(qe_ref, xa.at[pl.ds(0, rows)], X_IN + 0, at(dx=1))
    yag = (
        start(te_ref, ty.at[3], Y_AG + 0, yright),
        start(te_ref, ty.at[1], Y_AG + 1, yleft),
    )
    gather_b(0)
    cag = [start(te_ref, ty.at[4], C_AG + 0, core)]

    tz[0] = te_ref[...]
    ty[0] = te_ref[...]
    xa[pl.ds(rows, rows), :] = qe_ref[...]

    def project(parts):
        def forward(i):
            block = span(i, 256)
            left = jnp.concatenate([xa[pl.ds(p * rows, rows), :] for p in parts], axis=0)
            out = nn(left, head_ref[:, block]).astype(BF16)
            for n, p in enumerate(parts):
                qq[lax.div(i, 2), pl.ds((3 + p) * rows, rows), span(lax.rem(i, 2), 256)] = (
                    out[n * rows:(n + 1) * rows]
                )

        loop(feat // 256)(forward)

        def back(i):
            block = span(i, 256)
            total = 0.0
            for h in range(2):
                left = jnp.concatenate(
                    [qq[h, pl.ds((3 + p) * rows, rows), :] for p in parts], axis=0
                )
                total += nt(left, head_ref[block, pl.ds(h * fhalf, fhalf)])
            out = (scale * total).astype(BF16)
            for n, p in enumerate(parts):
                qp[pl.ds(p * rows, rows), block] = out[n * rows:(n + 1) * rows]

        loop(feat // 256)(back)

    def score_in(slot):
        s_in[:, pl.ds(slot * rows, rows)] = nt(qp[pl.ds(rows, 2 * rows), :], tz[slot])

    project([1])
    arrive(za[0])
    gather_a(1)
    arrive(yag)
    yag2 = (
        start(ty.at[3, lo], ty.at[2, lo], Y_AG + 2, yright),
        start(ty.at[1, hi], ty.at[2, hi], Y_AG + 3, yleft),
    )
    cag.append(start(ty.at[3], ty.at[7], C_AG + 1, core))
    cag.append(start(ty.at[1], ty.at[5], C_AG + 2, core))
    arrive(zb[0])
    gather_b(1)
    arrive(za[1])
    gather_a(2)
    arrive(yag2)
    cag.append(start(ty.at[2], ty.at[6], C_AG + 3, core))
    arrive(zb[1])
    gather_b(2)
    for one in (m1, m2, x1, x2):
        one.wait_recv()
    project([0, 2])
    arrive(za[2])
    gather_a(3)

    for p in range(3):
        wide[pl.ds(0, 8), :] = meta[p]
        info[pl.ds(p * rows, rows), :] = jnp.transpose(wide[...])
    for one in cag:
        one.wait_recv()

    def score_hard(i):
        s_hd[:, span(i, rows)] = nt(qp[pl.ds(0, 2 * rows), :], ty[i])

    loop(2 * NY)(score_hard)

    lane = lax.broadcasted_iota(jnp.int32, (1, cols), 1)
    slot_of, row_of = lane // rows, lane % rows
    other = slot_of // NY
    owner_core = c + other - 2 * c * other
    owner = (xl * NY + lax.rem(y + slot_of % NY, NY)) * 2 + owner_core
    hard_col = (owner * (2 * cols) + blk * rows + row_of).astype(F32)
    in_col = (xh * cols + lax.rem(z * rows + lane, cols)).astype(F32)

    def two_lanes(first, second):
        place = lax.broadcasted_iota(jnp.int32, (first.shape[0], 128), 1)
        return jnp.where(place == 0, first, second)

    def mask_hard(i):
        block = span(i, 32)
        named = info[block, :]
        count = jnp.zeros((32, cols), F32)
        for k in range(4):
            count += jnp.where(named[:, 2 + k:3 + k] == hard_col, 1.0, 0.0)
        kept = jnp.where(count > 0.0, s_hd[block, :] + jnp.log(jnp.maximum(count, 1.0)), NEG)
        top = jnp.max(kept, axis=1, keepdims=True)
        prob = jnp.exp(kept - top)
        s_hd[block, :] = prob
        st_hd[block, :] = two_lanes(top, jnp.sum(prob, axis=1, keepdims=True))

    loop(2 * rows // 32)(mask_hard)
    for slot in (0, 7, 1, 6, 2):
        score_in(slot)
    arrive(zb[2])
    for slot in (5, 3):
        score_in(slot)

    left, right = pl.ds(0, 4 * rows), pl.ds(5 * rows, 3 * rows)
    last_cols = pl.ds(4 * rows, rows)

    def stats_most(i):
        block = span(i, 32)
        one, two = s_in[block, left], s_in[block, right]
        top = jnp.maximum(
            jnp.max(one, axis=1, keepdims=True), jnp.max(two, axis=1, keepdims=True)
        )
        one, two = jnp.exp(one - top), jnp.exp(two - top)
        s_in[block, left] = one
        s_in[block, right] = two
        total = jnp.sum(one, axis=1, keepdims=True) + jnp.sum(two, axis=1, keepdims=True)
        st_in[block, pl.ds(0, 128)] = two_lanes(top, total)

    loop(2 * rows // 32)(stats_most)
    arrive(za[3])
    score_in(4)
    scores = s_in[:, last_cols]
    top = jnp.max(scores, axis=1, keepdims=True)
    prob = jnp.exp(scores - top)
    s_in[:, last_cols] = prob
    st_in[:, pl.ds(128, 128)] = two_lanes(top, jnp.sum(prob, axis=1, keepdims=True))

    place = lax.broadcasted_iota(jnp.int32, (rows, 128), 1)
    own, partner = pl.ds(0, rows), pl.ds(rows, rows)
    packed = jnp.zeros((rows, 128), F32)
    for where, value in enumerate((
        st_in[own, 0:1], st_in[own, 1:2], st_in[own, 128:129], st_in[own, 129:130],
        st_in[partner, 0:1], st_in[partner, 1:2], st_in[partner, 128:129], st_in[partner, 129:130],
        st_hd[partner, 0:1], st_hd[partner, 1:2], st_hd[own, 0:1], st_hd[own, 1:2],
    )):
        packed = jnp.where(place == where, value, packed)
    wide[...] = jnp.transpose(packed)

    def merge(parts):
        top = functools.reduce(jnp.maximum, [m for m, _ in parts])
        return top, sum(t * jnp.exp(m - top) for m, t in parts)

    def pair(ref, n):
        return ref[2 * n:2 * n + 1, :], ref[2 * n + 1:2 * n + 2, :]

    mine = merge([pair(wide, 0), pair(wide, 1), pair(wide, 4)])
    theirs = merge([pair(wide, 2), pair(wide, 3)])
    stat[0, 0:1, :], stat[0, 1:2, :] = mine
    stat[0, 2:3, :], stat[0, 3:4, :] = theirs
    stat[0, 4:6, :] = wide[10:12, :]
    stat[0, 6:8, :] = jnp.zeros((2, rows), F32)
    shared = [start(stat.at[0], stat.at[d], STAT + d - 1, at(dx=d)) for d in (1, 2, 3)]
    for one in shared:
        one.wait_recv()

    def log_total(parts):
        top, total = merge([pair(stat.at[d], n) for d, n in parts])
        return top + jnp.log(total)

    lse = [
        log_total([(0, 2), (1, 0), (3, 1)]),
        log_total([(0, 0), (1, 2), (2, 1)]),
        log_total([(0, 1), (2, 0), (3, 2)]),
    ]

    def factor(p, row):
        return meta[p, 0:1, :] * jnp.exp(wide[row:row + 1, :] - lse[p])

    factors = [
        factor(1, 0), factor(1, 2), factor(2, 4), factor(2, 6), factor(1, 8), factor(0, 10),
    ]
    for n, value in enumerate(factors):
        wide[n:n + 1, :] = value
    alpha[...] = jnp.transpose(wide[...])

    def grad_last(n):
        block = pl.ds(n * rows, rows)
        facts = info[pl.ds((1 + n) * rows, rows), :]
        hot = jnp.where(facts[:, 1:2] == in_col[:, 4 * rows:5 * rows], facts[:, 0:1], 0.0)
        a = alpha[:, 2 * n + 1:2 * n + 2]
        g_in[block, last_cols] = (a * s_in[block, last_cols] - hot).astype(BF16)

    grad_last(0)
    grad_last(1)

    def table_in(slot):
        return tn(g_in[:, pl.ds(slot * rows, rows)], qp[pl.ds(rows, 2 * rows), :])

    def table_pair(slot):
        both = tn(g_in[:, pl.ds(slot * rows, 2 * rows)], qp[pl.ds(rows, 2 * rows), :])
        zown[slot] = both[:rows]
        zown[slot + 1] = both[rows:]

    first = table_in(4).astype(BF16)
    zs[0, lo] = first[:half]
    zs[4, hi] = first[half:]
    ra, rb = {}, {}

    def reduce_a(k):
        ra[k] = (
            start(zs.at[k, lo], zr.at[k, lo], Z_RS + 2 * k, zright),
            start(zs.at[4 + k, hi], zr.at[4 + k, hi], Z_RS + 2 * k + 1, zleft),
        )

    def reduce_b(k):
        rb[k] = (
            start(zs.at[k, hi], zr.at[k, hi], Z_RS + 6 + 2 * k, zright),
            start(zs.at[4 + k, lo], zr.at[4 + k, lo], Z_RS + 7 + 2 * k, zleft),
        )

    def sum_a(k):
        arrive(ra[k])
        zs[k + 1, lo] = (zown[3 - k, lo] + zr[k, lo].astype(F32)).astype(BF16)
        zs[5 + k, hi] = (zown[5 + k, hi] + zr[4 + k, hi].astype(F32)).astype(BF16)
        reduce_a(k + 1)

    def sum_b(k):
        arrive(rb[k])
        zs[k + 1, hi] = (zown[3 - k, hi] + zr[k, hi].astype(F32)).astype(BF16)
        zs[5 + k, lo] = (zown[5 + k, lo] + zr[4 + k, lo].astype(F32)).astype(BF16)
        reduce_b(k + 1)

    reduce_a(0)

    def grad_most(n):
        def one(i):
            block = span(i, 32)
            low = pl.ds(pl.multiple_of(n * rows + i * 32, 32), 32)
            facts = info[pl.ds(pl.multiple_of((1 + n) * rows + i * 32, 32), 32), :]
            a, w, target = alpha[block, 2 * n:2 * n + 1], facts[:, 0:1], facts[:, 1:2]
            for part, begin, size in ((left, 0, 4 * rows), (right, 5 * rows, 3 * rows)):
                hot = jnp.where(target == in_col[:, begin:begin + size], w, 0.0)
                g_in[low, part] = (a * s_in[low, part] - hot).astype(BF16)

        loop(rows // 32)(one)

    grad_most(0)
    grad_most(1)

    def grad_hard(i):
        block = span(i, 32)
        g_hd[block, :] = (alpha[block, 5:6] * s_hd[block, :]).astype(BF16)
        low = pl.ds(pl.multiple_of(rows + i * 32, 32), 32)
        g_hd[low, :] = (alpha[block, 4:5] * s_hd[low, :]).astype(BF16)

    loop(rows // 32)(grad_hard)

    table_pair(2)
    table_pair(5)
    zs[1, hi] = zown[3, hi].astype(BF16)
    zs[5, lo] = zown[5, lo].astype(BF16)
    reduce_b(1)

    def ahead(i):
        block = span(i, 256)
        a_in, a_hd = jnp.zeros((2 * rows, 256), F32), jnp.zeros((2 * rows, 256), F32)
        for n in range(NZ // 2):
            part, two = pl.ds(2 * n * rows, 2 * rows), pl.ds(2 * n, 2)
            a_in += nn(g_in[:, part], tz[two, :, block].reshape(2 * rows, 256))
            a_hd += nn(g_hd[:, part], ty[two, :, block].reshape(2 * rows, 256))
        at0 = 3 * rows
        xa[pl.ds(at0, rows), block] = (scale * a_hd[:rows]).astype(BF16)
        xa[pl.ds(at0 + rows, rows), block] = (scale * (a_hd[rows:] + a_in[:rows])).astype(BF16)
        xa[pl.ds(at0 + 2 * rows, rows), block] = (scale * a_in[rows:]).astype(BF16)

    loop(feat // 256)(ahead)
    sum_a(0)

    def through(i):
        part = nn(xa[pl.ds(3 * rows, 3 * rows), :], head_ref[:, span(i, 256)])
        qq[lax.div(i, 2), pl.ds(0, 3 * rows), span(lax.rem(i, 2), 256)] = part.astype(BF16)
        acc[:, span(i, 256)] = part[rows:2 * rows]
        qgs[0, :, span(i, 256)] = part[:rows].astype(BF16)
        qgs[1, :, span(i, 256)] = part[2 * rows:].astype(BF16)

    loop(feat // 256)(through)
    back = (
        start(qgs.at[0], qgr.at[0], X_OUT + 0, at(dx=1)),
        start(qgs.at[1], qgr.at[1], X_OUT + 1, at(dx=2)),
    )
    sum_b(1)
    def head_part(which, out):
        def one(i):
            block = span(i, 256)
            out(block, tn(xa[:, block], qq[which]))
        loop(feat // 256)(one)

    def give(block, value):
        hcs[block, :] = value.astype(BF16)

    head_part(1 - c, give)
    hc = start(hcs, hcr, H_C, core)
    sum_a(1)

    def keep(block, value):
        h2[block, :] = value

    head_part(c, keep)
    zown[7] = table_in(7)
    table_pair(0)
    sum_b(2)
    hc.wait_recv()

    def join(i):
        block = span(i, 128)
        h2[block, :] = h2[block, :] + hcr[block, :].astype(F32)

    loop(feat // 128)(join)

    groups = feat // (8 * NY)
    view_a = h2.reshape(groups, NY, 8, fhalf)
    view_b = h2.reshape(2, NZ, 2, 8 * NY, fhalf)

    def cross_x(d):
        return (1 - xh if d & 2 else xh), (1 - xl if d & 1 else xl)

    stage1 = []
    for d in (1, 2, 3):
        there = lax.rem(y + d, NY)
        h1s[d - 1] = view_a[:, there, :, 0:fq].reshape(groups * 8, fq).astype(BF16)
        stage1.append(start(h1s.at[d - 1], h1r.at[d - 1], H_A1 + d - 1, at(dy=d)))
        xh2, xl2 = cross_x(d)
        h1s[d + 2] = view_b[xh2, :, xl2, :, fq:fhalf].reshape(groups * 8, fq).astype(BF16)
        stage1.append(start(h1s.at[d + 2], h1r.at[d + 2], H_B1 + d - 1, at(dx=d)))
    sum_a(2)

    def table_hard(i):
        return tn(g_hd[:, span(i, rows)], qp[pl.ds(0, 2 * rows), :])

    def cross(i):
        cs[i] = table_hard(NY + i).astype(BF16)

    loop(NY)(cross)
    crs = [start(cs.at[i], cr.at[i], C_RS + i, core) for i in range(NY)]
    for one in crs:
        one.wait_recv()

    def own_hard(i):
        yown[i] = table_hard(i) + cr[i].astype(F32)

    loop(NY)(own_hard)
    ys[0, lo] = yown[2, lo].astype(BF16)
    ys[1, hi] = yown[2, hi].astype(BF16)
    yrs = (
        start(ys.at[0, lo], yr.at[0, lo], Y_RS + 0, yright),
        start(ys.at[1, hi], yr.at[1, hi], Y_RS + 1, yleft),
    )

    hm[0] = view_a[:, y, :, 0:fq].reshape(groups * 8, fq)
    hm[1] = view_b[xh, :, xl, :, fq:fhalf].reshape(groups * 8, fq)
    for one in stage1:
        one.wait_recv()
    for n in range(2):
        hm[n] = (hm[n] + h1r[3 * n].astype(F32)) + (
            h1r[3 * n + 1].astype(F32) + h1r[3 * n + 2].astype(F32)
        )
    part_a = hm.at[0].reshape(2, NZ, 2, 8, fq)
    part_b = hm.at[1].reshape(NZ, NY, 8, fq)
    stage2 = []
    for d in (1, 2, 3):
        xh2, xl2 = cross_x(d)
        h2s[d - 1] = part_a[xh2, :, xl2].reshape(NZ * 8, fq).astype(BF16)
        stage2.append(start(h2s.at[d - 1], h2r.at[d - 1], H_A2 + d - 1, at(dx=d)))
        there = lax.rem(y + d, NY)
        h2s[d + 2] = part_b[:, there].reshape(NZ * 8, fq).astype(BF16)
        stage2.append(start(h2s.at[d + 2], h2r.at[d + 2], H_B2 + d - 1, at(dy=d)))
    arrive(yrs)
    ys[2, lo] = (yown[1, lo] + yr[0, lo].astype(F32)).astype(BF16)
    ys[2, hi] = yown[1, hi].astype(BF16)
    ys[3, lo] = yown[3, lo].astype(BF16)
    ys[3, hi] = (yown[3, hi] + yr[1, hi].astype(F32)).astype(BF16)
    yrs2 = (
        start(ys.at[2], yr.at[2], Y_RS + 2, yright),
        start(ys.at[3], yr.at[3], Y_RS + 3, yleft),
    )

    arrive(rb[3])
    for one in stage2:
        one.wait_recv()
    small_a = part_a[xh, :, xl].reshape(NZ * 8, fq)
    small_b = part_b[:, y].reshape(NZ * 8, fq)
    for d in range(3):
        small_a = small_a + h2r[d].astype(F32)
        small_b = small_b + h2r[d + 3].astype(F32)
    hzs[:, :, pl.ds(0, fq)] = small_a.reshape(NZ, 8, fq)
    hzs[:, :, pl.ds(fq, fq)] = small_b.reshape(NZ, 8, fq)
    hz = [
        start(hzs.at[lax.rem(z + d, NZ)], hzr.at[d - 1], H_Z + d - 1, at(dz=d))
        for d in range(1, NZ)
    ]

    arrive(back)
    acc[...] = acc[...] + qgr[0].astype(F32) + qgr[1].astype(F32)

    def question(i):
        block = span(i, 256)
        gq_ref[:, block] = nt(acc[...].astype(BF16), head_ref[block, :]).astype(BF16)

    loop(feat // 256)(question)

    for one in hz:
        one.wait_recv()
    last = hzs[z]
    for d in range(NZ - 1):
        last = last + hzr[d]
    hc2s[...] = last
    hc2 = start(hc2s, hc2r, H_C2, core)

    arrive(yrs2)
    zown[0] = (zown[0] + yown[0]) + (yr[2].astype(F32) + yr[3].astype(F32))
    arrive(ra[3])
    gt_ref[...] = (zown[0] + (zr[3].astype(F32) + zr[7].astype(F32))).astype(BF16)

    hc2.wait_recv()
    far = hc2r[...]
    picked_own = jnp.where(c == 0, last[0:4], last[4:8])
    picked = jnp.where(c == 0, far[0:4], far[4:8])
    gh_ref[:, pl.ds(0, fhalf)] = jnp.where(c == 0, picked_own, picked)
    gh_ref[:, pl.ds(fhalf, fhalf)] = jnp.where(c == 0, picked, picked_own)

    for one in started:
        one.wait_send()


def hand_over(*refs):
    for source, target in zip(refs[:3], refs[3:]):
        target[...] = source[...]


def body(q_embed, t_embed, head, positive, hard_ids, loss_weight):
    rows, feat = q_embed.shape[1:]
    cols, fhalf, fq = NZ * rows, feat // 2, feat // 4
    vmem = pl.BlockSpec(memory_space=pltpu.VMEM)
    shapes = [
        ((6 * rows, feat), BF16),
        ((2, 6 * rows, fhalf), BF16),
        ((3 * rows, feat), BF16),
        ((NZ, rows, feat), BF16),
        ((2 * NY, rows, feat), BF16),
        ((3, 8, rows), F32),
        ((3 * rows, 128), F32),
        ((2 * rows, cols), F32),
        ((2 * rows, cols), F32),
        ((2 * rows, cols), BF16),
        ((2 * rows, cols), BF16),
        ((2 * rows, 256), F32),
        ((2 * rows, 128), F32),
        ((4, 8, rows), F32),
        ((128, rows), F32),
        ((rows, 128), F32),
        ((8, rows, feat), BF16),
        ((8, rows, feat), BF16),
        ((8, rows, feat), F32),
        ((NY, rows, feat), BF16),
        ((NY, rows, feat), BF16),
        ((NY, rows, feat), F32),
        ((4, rows, feat), BF16),
        ((4, rows, feat), BF16),
        ((rows, feat), F32),
        ((2, rows, feat), BF16),
        ((2, rows, feat), BF16),
        ((feat, fhalf), F32),
        ((feat, fhalf), BF16),
        ((feat, fhalf), BF16),
        ((6, feat // NY, fq), BF16),
        ((6, feat // NY, fq), BF16),
        ((2, feat // NY, fq), F32),
        ((6, NZ * 8, fq), BF16),
        ((6, NZ * 8, fq), BF16),
        ((NZ, 8, fhalf), F32),
        ((NZ - 1, 8, fhalf), F32),
        ((8, fhalf), F32),
        ((8, fhalf), F32),
    ]
    outs = (
        jax.ShapeDtypeStruct((rows, feat), BF16),
        jax.ShapeDtypeStruct((rows, feat), BF16),
        jax.ShapeDtypeStruct((4, feat), F32),
    )
    results = pl.pallas_call(
        kernel,
        out_shape=outs,
        in_specs=[vmem] * 6,
        out_specs=(vmem, vmem, vmem),
        scratch_shapes=[pltpu.VMEM(s, t) for s, t in shapes] + [
            pltpu.SemaphoreType.DMA((COPIES,)),
            pltpu.SemaphoreType.DMA((COPIES,)),
        ],
        compiler_params=pltpu.CompilerParams(
            collective_id=0, has_side_effects=True, vmem_limit_bytes=56 * 1024 * 1024
        ),
    )(q_embed[0], t_embed[0], head, loss_weight, positive, hard_ids[0].T)
    grad_q, grad_t, grad_head = pl.pallas_call(
        hand_over,
        out_shape=outs,
        in_specs=[vmem] * 3,
        out_specs=(vmem, vmem, vmem),
    )(*results)
    return (grad_q[None], grad_t[None], grad_head)


def solution(mesh):
    in_specs = (
        P("group", "blk", None),
        P("group", "blk", None),
        P(),
        P("group", "blk"),
        P("group", "blk", None),
        P("group", "blk"),
    )
    out_specs = (P("group", "blk", None), P("group", "blk", None), P(("blk", "group"), None))
    return jax.shard_map(body, mesh=mesh, in_specs=in_specs, out_specs=out_specs, check_vma=False)
```

```python
import functools
import math

import jax
import jax.numpy as jnp
from jax import lax
from jax.experimental import pallas as pl
from jax.experimental.pallas import tpu as pltpu
from jax.sharding import PartitionSpec as P

MESH = pl.DeviceIdType.MESH
F32 = jnp.float32
BF16 = jnp.bfloat16

NZ = 8
NY = 4
NEG = -1e30


Z_AG, Y_AG, C_AG, X_IN, STAT = 0, 14, 18, 22, 26
Z_RS, C_RS, Y_RS, X_OUT = 29, 43, 47, 51
H_IN, H_A1, H_B1, H_A2, H_B2, H_Z = 53, 57, 60, 63, 66, 69
COPIES = 84


def nn(left, right):
    return lax.dot_general(left, right, (((1,), (0,)), ((), ())), preferred_element_type=F32)


def nt(left, right):
    return lax.dot_general(left, right, (((1,), (1,)), ((), ())), preferred_element_type=F32)


def tn(left, right):
    return lax.dot_general(left, right, (((0,), (0,)), ((), ())), preferred_element_type=F32)


def span(i, size):
    return pl.ds(pl.multiple_of(i * size, size), size)


def loop(count, unroll=1):
    def run(step):
        lax.fori_loop(0, count, lambda i, carry: (step(i), carry)[1], 0, unroll=unroll)
    return run


def kernel(
    qe_ref, te_ref, head_ref, weight_ref, positive_ref, ids_ref, gq_ref, gt_ref, gh_ref,
    xa, qq, qp, tz, ty, meta, info, s_in, s_hd, g_in, g_hd, st_in, st_hd, stat, wide, alpha,
    zs, zr, zown, cs, cr, yown, ys, yr, acc, ar,
    h2, xap, qqp, h1s, h1r, hm, h2s, h2r, hzs, hzr,
    send_sem, recv_sem,
):
    rows, feat = qe_ref.shape
    half = rows // 2
    scale = feat ** -0.5
    cols = NZ * rows
    fhalf, fq = feat // 2, feat // 4
    blk, grp = lax.axis_index("blk"), lax.axis_index("group")
    xh, z = lax.div(blk, NZ), lax.rem(blk, NZ)
    xl, y, c = lax.div(grp, 2 * NY), lax.rem(lax.div(grp, 2), NY), lax.rem(grp, 2)

    def at(dz=0, dy=0, dx=0, dc=0):
        xh2 = 1 - xh if dx & 2 else xh
        xl2 = 1 - xl if dx & 1 else xl
        c2 = 1 - c if dc else c
        z2, y2 = lax.rem(z + dz + NZ, NZ), lax.rem(y + dy + NY, NY)
        return (xh2 * NZ + z2, (xl2 * NY + y2) * 2 + c2)

    def copy(src, dst, sem, device):
        return pltpu.make_async_remote_copy(
            src_ref=src, dst_ref=dst, send_sem=send_sem.at[sem], recv_sem=recv_sem.at[sem],
            device_id=device, device_id_type=MESH,
        )

    peers = (
        [at(dz=d) for d in (1, -1)] + [at(dy=d) for d in (1, -1)]
        + [at(dx=d) for d in (1, 2, 3)] + [at(dc=1)]
    )
    barrier = pltpu.get_barrier_semaphore()
    for peer in peers:
        pl.semaphore_signal(barrier, inc=1, device_id=peer, device_id_type=MESH)

    meta[1, 0:1, :] = weight_ref[...]
    meta[1, 1:2, :] = positive_ref[...].astype(F32)
    meta[1, 2:6, :] = ids_ref[...].astype(F32)
    meta[1, 6:8, :] = jnp.zeros((2, rows), F32)
    pl.semaphore_wait(barrier, len(peers))

    started = []

    def start(*args):
        one = copy(*args)
        one.start()
        started.append(one)
        return one

    zright, zleft = at(dz=1), at(dz=-1)
    yright, yleft = at(dy=1), at(dy=-1)
    core = at(dc=1)
    lo, hi = pl.ds(0, half), pl.ds(half, half)

    za, zb = {}, {}

    def gather_a(k):
        src = (te_ref.at[lo], te_ref.at[hi]) if k == 0 else (tz.at[NZ - k, lo], tz.at[k, hi])
        za[k] = (
            start(src[0], tz.at[NZ - 1 - k, lo], Z_AG + 2 * k, zright),
            start(src[1], tz.at[1 + k, hi], Z_AG + 2 * k + 1, zleft),
        )

    def gather_b(k):
        src = (te_ref.at[hi], te_ref.at[lo]) if k == 0 else (tz.at[NZ - k, hi], tz.at[k, lo])
        zb[k] = (
            start(src[0], tz.at[NZ - 1 - k, hi], Z_AG + 8 + 2 * k, zright),
            start(src[1], tz.at[1 + k, lo], Z_AG + 9 + 2 * k, zleft),
        )

    def arrive(pair):
        pair[0].wait_recv()
        pair[1].wait_recv()

    gather_a(0)
    m2 = start(meta.at[1], meta.at[2], X_IN + 3, at(dx=2))
    m1 = start(meta.at[1], meta.at[0], X_IN + 2, at(dx=1))
    x2 = start(qe_ref, xa.at[pl.ds(2 * rows, rows)], X_IN + 1, at(dx=2))
    x1 = start(qe_ref, xa.at[pl.ds(0, rows)], X_IN + 0, at(dx=1))
    yag = (
        start(te_ref, ty.at[3], Y_AG + 0, yright),
        start(te_ref, ty.at[1], Y_AG + 1, yleft),
    )
    gather_b(0)
    cag = [start(te_ref, ty.at[4], C_AG + 0, core)]

    tz[0] = te_ref[...]
    ty[0] = te_ref[...]
    xa[pl.ds(rows, rows), :] = qe_ref[...]

    def project(parts):
        def one(i):
            block = span(i, 256)
            left = jnp.concatenate([xa[pl.ds(p * rows, rows), :] for p in parts], axis=0)
            out = nn(left, head_ref[:, block]).astype(BF16)
            for n, p in enumerate(parts):
                qq[lax.div(i, 2), pl.ds((3 + p) * rows, rows), span(lax.rem(i, 2), 256)] = (
                    out[n * rows:(n + 1) * rows]
                )

        loop(feat // 256)(one)

    def project_back(parts):
        def one(i):
            block = span(i, 256)
            total = 0.0
            for h in range(2):
                left = jnp.concatenate(
                    [qq[h, pl.ds((3 + p) * rows, rows), :] for p in parts], axis=0
                )
                total += nt(left, head_ref[block, pl.ds(h * fhalf, fhalf)])
            out = (scale * total).astype(BF16)
            for n, p in enumerate(parts):
                qp[pl.ds(p * rows, rows), block] = out[n * rows:(n + 1) * rows]

        loop(feat // 256)(one)

    low, high, top_rows = pl.ds(0, rows), pl.ds(rows, rows), pl.ds(2 * rows, rows)

    def score_in(slot, where, what):
        s_in[where, pl.ds(slot * rows, rows)] = nt(qp[what, :], tz[slot])

    project([1])
    project_back([1])
    m1.wait_recv()
    m2.wait_recv()
    for p in range(3):
        wide[pl.ds(0, 8), :] = meta[p]
        info[pl.ds(p * rows, rows), :] = jnp.transpose(wide[...])

    lane = lax.broadcasted_iota(jnp.int32, (1, cols), 1)
    slot_of, row_of = lane // rows, lane % rows
    other = slot_of // NY
    owner_core = c + other - 2 * c * other
    owner = (xl * NY + lax.rem(y + slot_of % NY, NY)) * 2 + owner_core
    hard_col = (owner * (2 * cols) + blk * rows + row_of).astype(F32)
    in_col = (xh * cols + lax.rem(z * rows + lane, cols)).astype(F32)

    def mask_hard(i):
        block = span(i, 32)
        named = info[block, :]
        count = jnp.zeros((32, cols), F32)
        for k in range(4):
            count += jnp.where(named[:, 2 + k:3 + k] == hard_col, 1.0, 0.0)
        s_hd[block, :] = jnp.where(count > 0.0, jnp.log(jnp.maximum(count, 1.0)), NEG)

    arrive(za[0])
    gather_a(1)
    loop(rows // 32)(mask_hard)
    arrive(zb[0])
    gather_b(1)
    arrive(yag)
    yag2 = (
        start(ty.at[3, lo], ty.at[2, lo], Y_AG + 2, yright),
        start(ty.at[1, hi], ty.at[2, hi], Y_AG + 3, yleft),
    )
    cag.append(start(ty.at[3], ty.at[7], C_AG + 1, core))
    cag.append(start(ty.at[1], ty.at[5], C_AG + 2, core))
    loop(rows // 32)(lambda i: mask_hard(i + rows // 32))
    arrive(za[1])
    gather_a(2)
    arrive(yag2)
    cag.append(start(ty.at[2], ty.at[6], C_AG + 3, core))
    arrive(zb[1])
    gather_b(2)

    def score_hard(where):
        def one(i):
            block = span(i, rows)
            s_hd[where, block] = s_hd[where, block] + nt(qp[where, :], ty[i])
        loop(2 * NY)(one)

    def two_lanes(first, second):
        place = lax.broadcasted_iota(jnp.int32, (first.shape[0], 128), 1)
        return jnp.where(place == 0, first, second)

    def stats_hard(i):
        block = span(i, 32)
        kept = s_hd[block, :]
        top = jnp.max(kept, axis=1, keepdims=True)
        prob = jnp.exp(kept - top)
        s_hd[block, :] = prob
        st_hd[block, :] = two_lanes(top, jnp.sum(prob, axis=1, keepdims=True))

    for one in cag:
        one.wait_recv()
    arrive(za[2])
    gather_a(3)
    score_hard(high)
    loop(rows // 32)(lambda i: stats_hard(i + rows // 32))
    for slot in (0, 7, 1, 6, 2):
        score_in(slot, low, high)
    x1.wait_recv()
    x2.wait_recv()
    early, late = pl.ds(0, 3 * rows), pl.ds(3 * rows, 3 * rows)
    operands = [start(xa.at[early], xap.at[early], H_IN + 0, core)]
    project([0, 2])
    operands.append(start(qq.at[1 - c, late], qqp.at[late], H_IN + 1, core))
    project_back([0, 2])
    score_hard(low)
    loop(rows // 32)(stats_hard)
    for slot in (0, 7, 1, 6, 2):
        score_in(slot, high, top_rows)
    arrive(zb[2])
    for slot in (5, 3):
        score_in(slot, pl.ds(0, 2 * rows), pl.ds(rows, 2 * rows))

    left, right = pl.ds(0, 4 * rows), pl.ds(5 * rows, 3 * rows)
    last_cols = pl.ds(4 * rows, rows)

    def stats_most(i):
        block = span(i, 32)
        one, two = s_in[block, left], s_in[block, right]
        top = jnp.maximum(
            jnp.max(one, axis=1, keepdims=True), jnp.max(two, axis=1, keepdims=True)
        )
        one, two = jnp.exp(one - top), jnp.exp(two - top)
        s_in[block, left] = one
        s_in[block, right] = two
        total = jnp.sum(one, axis=1, keepdims=True) + jnp.sum(two, axis=1, keepdims=True)
        st_in[block, pl.ds(0, 128)] = two_lanes(top, total)

    loop(2 * rows // 32)(stats_most)
    arrive(za[3])
    score_in(4, pl.ds(0, 2 * rows), pl.ds(rows, 2 * rows))
    scores = s_in[:, last_cols]
    top = jnp.max(scores, axis=1, keepdims=True)
    prob = jnp.exp(scores - top)
    s_in[:, last_cols] = prob
    st_in[:, pl.ds(128, 128)] = two_lanes(top, jnp.sum(prob, axis=1, keepdims=True))

    place = lax.broadcasted_iota(jnp.int32, (rows, 128), 1)
    own, partner = pl.ds(0, rows), pl.ds(rows, rows)
    packed = jnp.zeros((rows, 128), F32)
    for where, value in enumerate((
        st_in[own, 0:1], st_in[own, 1:2], st_in[own, 128:129], st_in[own, 129:130],
        st_in[partner, 0:1], st_in[partner, 1:2], st_in[partner, 128:129], st_in[partner, 129:130],
        st_hd[partner, 0:1], st_hd[partner, 1:2], st_hd[own, 0:1], st_hd[own, 1:2],
    )):
        packed = jnp.where(place == where, value, packed)
    wide[...] = jnp.transpose(packed)

    def merge(parts):
        top = functools.reduce(jnp.maximum, [m for m, _ in parts])
        return top, sum(t * jnp.exp(m - top) for m, t in parts)

    def pair(ref, n):
        return ref[2 * n:2 * n + 1, :], ref[2 * n + 1:2 * n + 2, :]

    mine = merge([pair(wide, 0), pair(wide, 1), pair(wide, 4)])
    theirs = merge([pair(wide, 2), pair(wide, 3)])
    stat[0, 0:1, :], stat[0, 1:2, :] = mine
    stat[0, 2:3, :], stat[0, 3:4, :] = theirs
    stat[0, 4:6, :] = wide[10:12, :]
    stat[0, 6:8, :] = jnp.zeros((2, rows), F32)
    shared = [start(stat.at[0], stat.at[d], STAT + d - 1, at(dx=d)) for d in (1, 2, 3)]
    for one in shared:
        one.wait_recv()

    def log_total(parts):
        top, total = merge([pair(stat.at[d], n) for d, n in parts])
        return top + jnp.log(total)

    lse = [
        log_total([(0, 2), (1, 0), (3, 1)]),
        log_total([(0, 0), (1, 2), (2, 1)]),
        log_total([(0, 1), (2, 0), (3, 2)]),
    ]

    def factor(p, row):
        return meta[p, 0:1, :] * jnp.exp(wide[row:row + 1, :] - lse[p])

    factors = [
        factor(1, 0), factor(1, 2), factor(2, 4), factor(2, 6), factor(1, 8), factor(0, 10),
    ]
    for n, value in enumerate(factors):
        wide[n:n + 1, :] = value
    alpha[...] = jnp.transpose(wide[...])

    def grad_last(n):
        block = pl.ds(n * rows, rows)
        facts = info[pl.ds((1 + n) * rows, rows), :]
        hot = jnp.where(facts[:, 1:2] == in_col[:, 4 * rows:5 * rows], facts[:, 0:1], 0.0)
        a = alpha[:, 2 * n + 1:2 * n + 2]
        g_in[block, last_cols] = (a * s_in[block, last_cols] - hot).astype(BF16)

    grad_last(0)
    grad_last(1)

    def table_in(slot):
        return tn(g_in[:, pl.ds(slot * rows, rows)], qp[pl.ds(rows, 2 * rows), :])

    def table_pair(slot):
        both = tn(g_in[:, pl.ds(slot * rows, 2 * rows)], qp[pl.ds(rows, 2 * rows), :])
        zown[slot] = both[:rows]
        zown[slot + 1] = both[rows:]

    first = table_in(4).astype(BF16)
    zs[0, lo] = first[:half]
    zs[4, hi] = first[half:]
    ra, rb = {}, {}

    def reduce_a(k):
        ra[k] = (
            start(zs.at[k, lo], zr.at[k, lo], Z_RS + 2 * k, zright),
            start(zs.at[4 + k, hi], zr.at[4 + k, hi], Z_RS + 2 * k + 1, zleft),
        )

    def reduce_b(k):
        rb[k] = (
            start(zs.at[k, hi], zr.at[k, hi], Z_RS + 6 + 2 * k, zright),
            start(zs.at[4 + k, lo], zr.at[4 + k, lo], Z_RS + 7 + 2 * k, zleft),
        )

    def sum_a(k):
        arrive(ra[k])
        zs[k + 1, lo] = (zown[3 - k, lo] + zr[k, lo].astype(F32)).astype(BF16)
        zs[5 + k, hi] = (zown[5 + k, hi] + zr[4 + k, hi].astype(F32)).astype(BF16)
        reduce_a(k + 1)

    def sum_b(k):
        arrive(rb[k])
        zs[k + 1, hi] = (zown[3 - k, hi] + zr[k, hi].astype(F32)).astype(BF16)
        zs[5 + k, lo] = (zown[5 + k, lo] + zr[4 + k, lo].astype(F32)).astype(BF16)
        reduce_b(k + 1)

    reduce_a(0)

    def grad_most(n):
        def one(i):
            block = span(i, 32)
            place = pl.ds(pl.multiple_of(n * rows + i * 32, 32), 32)
            facts = info[pl.ds(pl.multiple_of((1 + n) * rows + i * 32, 32), 32), :]
            a, w, target = alpha[block, 2 * n:2 * n + 1], facts[:, 0:1], facts[:, 1:2]
            for part, begin, size in ((left, 0, 4 * rows), (right, 5 * rows, 3 * rows)):
                hot = jnp.where(target == in_col[:, begin:begin + size], w, 0.0)
                g_in[place, part] = (a * s_in[place, part] - hot).astype(BF16)

        loop(rows // 32)(one)

    grad_most(0)
    grad_most(1)

    def grad_hard(i):
        block = span(i, 32)
        g_hd[block, :] = (alpha[block, 5:6] * s_hd[block, :]).astype(BF16)
        place = pl.ds(pl.multiple_of(rows + i * 32, 32), 32)
        g_hd[place, :] = (alpha[block, 4:5] * s_hd[place, :]).astype(BF16)

    loop(rows // 32)(grad_hard)

    table_pair(2)
    table_pair(5)
    zs[1, hi] = zown[3, hi].astype(BF16)
    zs[5, lo] = zown[5, lo].astype(BF16)
    reduce_b(1)

    def table_hard(first):
        many = tn(g_hd[:, pl.ds(first * rows, NY * rows)], qp[pl.ds(0, 2 * rows), :])
        return many.reshape(NY, rows, feat)

    cs[...] = table_hard(NY).astype(BF16)
    cross = start(cs, cr, C_RS, core)

    def ahead(i):
        block = span(i, 256)
        a_in, a_hd = jnp.zeros((2 * rows, 256), F32), jnp.zeros((2 * rows, 256), F32)
        for n in range(NZ // 2):
            part, two = pl.ds(2 * n * rows, 2 * rows), pl.ds(2 * n, 2)
            a_in += nn(g_in[:, part], tz[two, :, block].reshape(2 * rows, 256))
            a_hd += nn(g_hd[:, part], ty[two, :, block].reshape(2 * rows, 256))
        at0 = 3 * rows
        xa[pl.ds(at0, rows), block] = (scale * a_hd[:rows]).astype(BF16)
        own_part = scale * (a_hd[rows:] + a_in[:rows])
        acc[:, block] = own_part
        xa[pl.ds(at0 + rows, rows), block] = own_part.astype(BF16)
        xa[pl.ds(at0 + 2 * rows, rows), block] = (scale * a_in[rows:]).astype(BF16)

    loop(feat // 256)(ahead)
    back = (
        start(xa.at[pl.ds(3 * rows, rows)], ar.at[0], X_OUT + 0, at(dx=1)),
        start(xa.at[pl.ds(5 * rows, rows)], ar.at[1], X_OUT + 1, at(dx=2)),
    )
    operands.append(start(xa.at[late], xap.at[late], H_IN + 2, core))
    def through(i):
        part = nn(xa[pl.ds(3 * rows, 3 * rows), :], head_ref[:, span(i, 256)])
        qq[lax.div(i, 2), pl.ds(0, 3 * rows), span(lax.rem(i, 2), 256)] = part.astype(BF16)

    loop(feat // 256)(through)
    operands.append(start(qq.at[1 - c, early], qqp.at[early], H_IN + 3, core))
    sum_a(0)
    sum_b(1)
    cross.wait_recv()
    yown[...] = table_hard(0) + cr[...].astype(F32)
    ys[0, lo] = yown[2, lo].astype(BF16)
    ys[1, hi] = yown[2, hi].astype(BF16)
    yrs = (
        start(ys.at[0, lo], yr.at[0, lo], Y_RS + 0, yright),
        start(ys.at[1, hi], yr.at[1, hi], Y_RS + 1, yleft),
    )
    zown[7] = table_in(7)
    table_pair(0)
    for one in operands:
        one.wait_recv()

    def head_part(i):
        block = span(i, 256)
        h2[block, :] = tn(xa[:, block], qq[c]) + tn(xap[:, block], qqp[...])

    loop(feat // 256)(head_part)

    groups = feat // (8 * NY)
    view_a = h2.reshape(groups, NY, 8, fhalf)
    view_b = h2.reshape(2, NZ, 2, 8 * NY, fhalf)

    def cross_x(d):
        return (1 - xh if d & 2 else xh), (1 - xl if d & 1 else xl)

    stage1 = []
    for d in (1, 2, 3):
        there = lax.rem(y + d, NY)
        h1s[d - 1] = view_a[:, there, :, 0:fq].reshape(groups * 8, fq).astype(BF16)
        stage1.append(start(h1s.at[d - 1], h1r.at[d - 1], H_A1 + d - 1, at(dy=d)))
        xh2, xl2 = cross_x(d)
        h1s[d + 2] = view_b[xh2, :, xl2, :, fq:fhalf].reshape(groups * 8, fq).astype(BF16)
        stage1.append(start(h1s.at[d + 2], h1r.at[d + 2], H_B1 + d - 1, at(dx=d)))
    sum_a(1)
    sum_b(2)

    hm[0] = view_a[:, y, :, 0:fq].reshape(groups * 8, fq)
    hm[1] = view_b[xh, :, xl, :, fq:fhalf].reshape(groups * 8, fq)
    sum_a(2)
    for one in stage1:
        one.wait_recv()
    for n in range(2):
        hm[n] = (hm[n] + h1r[3 * n].astype(F32)) + (
            h1r[3 * n + 1].astype(F32) + h1r[3 * n + 2].astype(F32)
        )
    part_a = hm.at[0].reshape(2, NZ, 2, 8, fq)
    part_b = hm.at[1].reshape(NZ, NY, 8, fq)
    stage2 = []
    for d in (1, 2, 3):
        xh2, xl2 = cross_x(d)
        h2s[d - 1] = part_a[xh2, :, xl2].reshape(NZ * 8, fq).astype(BF16)
        stage2.append(start(h2s.at[d - 1], h2r.at[d - 1], H_A2 + d - 1, at(dx=d)))
        there = lax.rem(y + d, NY)
        h2s[d + 2] = part_b[:, there].reshape(NZ * 8, fq).astype(BF16)
        stage2.append(start(h2s.at[d + 2], h2r.at[d + 2], H_B2 + d - 1, at(dy=d)))
    arrive(yrs)
    ys[2, lo] = (yown[1, lo] + yr[0, lo].astype(F32)).astype(BF16)
    ys[2, hi] = yown[1, hi].astype(BF16)
    ys[3, lo] = yown[3, lo].astype(BF16)
    ys[3, hi] = (yown[3, hi] + yr[1, hi].astype(F32)).astype(BF16)
    yrs2 = (
        start(ys.at[2], yr.at[2], Y_RS + 2, yright),
        start(ys.at[3], yr.at[3], Y_RS + 3, yleft),
    )
    for one in stage2:
        one.wait_recv()
    small_a = part_a[xh, :, xl].reshape(NZ * 8, fq)
    small_b = part_b[:, y].reshape(NZ * 8, fq)
    for d in range(3):
        small_a = small_a + h2r[d].astype(F32)
        small_b = small_b + h2r[d + 3].astype(F32)
    hzs[:, :, pl.ds(0, fq)] = small_a.reshape(NZ, 8, fq)
    hzs[:, :, pl.ds(fq, fq)] = small_b.reshape(NZ, 8, fq)
    hz = [start(hzs.at[z], hzr.at[1, NZ - 1], H_Z + 2 * NZ - 2, core)]
    for d in (4, 3, 5, 2, 6, 1, 7):
        there = hzs.at[lax.rem(z + d, NZ)]
        hz.append(start(there, hzr.at[0, d - 1], H_Z + d - 1, at(dz=d)))
        hz.append(start(there, hzr.at[1, d - 1], H_Z + NZ - 2 + d, at(dz=d, dc=1)))

    arrive(back)
    acc[...] = acc[...] + ar[0].astype(F32) + ar[1].astype(F32)

    def question_in(i):
        block = span(i, 256)
        ar[0, :, block] = nn(acc[...].astype(BF16), head_ref[:, block]).astype(BF16)

    def question(i):
        block = span(i, 256)
        gq_ref[:, block] = nt(ar[0], head_ref[block, :]).astype(BF16)

    loop(feat // 256)(question_in)
    loop(feat // 256)(question)

    arrive(rb[3])
    arrive(yrs2)
    zown[0] = (zown[0] + yown[0]) + (yr[2].astype(F32) + yr[3].astype(F32))
    arrive(ra[3])
    gt_ref[...] = (zown[0] + (zr[3].astype(F32) + zr[7].astype(F32))).astype(BF16)

    for one in hz:
        one.wait_recv()
    near, far = hzs[z], hzr[1, NZ - 1]
    for d in range(NZ - 1):
        near, far = near + hzr[0, d], far + hzr[1, d]
    near = jnp.where(c == 0, near[0:4], near[4:8])
    far = jnp.where(c == 0, far[0:4], far[4:8])
    gh_ref[:, pl.ds(0, fhalf)] = jnp.where(c == 0, near, far)
    gh_ref[:, pl.ds(fhalf, fhalf)] = jnp.where(c == 0, far, near)

    for one in started:
        one.wait_send()


def hand_over(*refs):
    for source, target in zip(refs[:3], refs[3:]):
        target[...] = source[...]


def body(q_embed, t_embed, head, positive, hard_ids, loss_weight):
    rows, feat = q_embed.shape[1:]
    cols, fhalf, fq = NZ * rows, feat // 2, feat // 4
    vmem = pl.BlockSpec(memory_space=pltpu.VMEM)
    shapes = [
        ((6 * rows, feat), BF16),
        ((2, 6 * rows, fhalf), BF16),
        ((3 * rows, feat), BF16),
        ((NZ, rows, feat), BF16),
        ((2 * NY, rows, feat), BF16),
        ((3, 8, rows), F32),
        ((3 * rows, 128), F32),
        ((2 * rows, cols), F32),
        ((2 * rows, cols), F32),
        ((2 * rows, cols), BF16),
        ((2 * rows, cols), BF16),
        ((2 * rows, 256), F32),
        ((2 * rows, 128), F32),
        ((4, 8, rows), F32),
        ((128, rows), F32),
        ((rows, 128), F32),
        ((8, rows, feat), BF16),
        ((8, rows, feat), BF16),
        ((8, rows, feat), F32),
        ((NY, rows, feat), BF16),
        ((NY, rows, feat), BF16),
        ((NY, rows, feat), F32),
        ((4, rows, feat), BF16),
        ((4, rows, feat), BF16),
        ((rows, feat), F32),
        ((2, rows, feat), BF16),
        ((feat, fhalf), F32),
        ((6 * rows, feat), BF16),
        ((6 * rows, fhalf), BF16),
        ((6, feat // NY, fq), BF16),
        ((6, feat // NY, fq), BF16),
        ((2, feat // NY, fq), F32),
        ((6, NZ * 8, fq), BF16),
        ((6, NZ * 8, fq), BF16),
        ((NZ, 8, fhalf), F32),
        ((2, NZ, 8, fhalf), F32),
    ]
    outs = (
        jax.ShapeDtypeStruct((rows, feat), BF16),
        jax.ShapeDtypeStruct((rows, feat), BF16),
        jax.ShapeDtypeStruct((4, feat), F32),
    )
    results = pl.pallas_call(
        kernel,
        out_shape=outs,
        in_specs=[vmem] * 6,
        out_specs=(vmem, vmem, vmem),
        scratch_shapes=[pltpu.VMEM(s, t) for s, t in shapes] + [
            pltpu.SemaphoreType.DMA((COPIES,)),
            pltpu.SemaphoreType.DMA((COPIES,)),
        ],
        compiler_params=pltpu.CompilerParams(
            collective_id=0, has_side_effects=True, vmem_limit_bytes=56 * 1024 * 1024
        ),
    )(q_embed[0], t_embed[0], head, loss_weight, positive, hard_ids[0].T)
    grad_q, grad_t, grad_head = pl.pallas_call(
        hand_over,
        out_shape=outs,
        in_specs=[vmem] * 3,
        out_specs=(vmem, vmem, vmem),
    )(*results)
    return (grad_q[None], grad_t[None], grad_head)


def solution(mesh):
    in_specs = (
        P("group", "blk", None),
        P("group", "blk", None),
        P(),
        P("group", "blk"),
        P("group", "blk", None),
        P("group", "blk"),
    )
    out_specs = (P("group", "blk", None), P("group", "blk", None), P(("blk", "group"), None))
    return jax.shard_map(body, mesh=mesh, in_specs=in_specs, out_specs=out_specs, check_vma=False)
```

```python
import functools
import math

import jax
import jax.numpy as jnp
from jax import lax
from jax.experimental import pallas as pl
from jax.experimental.pallas import tpu as pltpu
from jax.sharding import PartitionSpec as P

MESH = pl.DeviceIdType.MESH
F32 = jnp.float32
BF16 = jnp.bfloat16

NZ = 8
NY = 4
NEG = -1e30


Z_AG, Y_AG, C_AG, X_IN, STAT = 0, 14, 18, 22, 26
Z_RS, C_RS, Y_RS, X_OUT = 29, 43, 47, 51
H_IN, H_A1, H_B1, H_A2, H_B2, H_Z = 53, 57, 60, 63, 66, 69
COPIES = 84


def nn(left, right):
    return lax.dot_general(left, right, (((1,), (0,)), ((), ())), preferred_element_type=F32)


def nt(left, right):
    return lax.dot_general(left, right, (((1,), (1,)), ((), ())), preferred_element_type=F32)


def tn(left, right):
    return lax.dot_general(left, right, (((0,), (0,)), ((), ())), preferred_element_type=F32)


def span(i, size):
    return pl.ds(pl.multiple_of(i * size, size), size)


def loop(count, unroll=1):
    def run(step):
        lax.fori_loop(0, count, lambda i, carry: (step(i), carry)[1], 0, unroll=unroll)
    return run


def kernel(
    qe_ref, te_ref, head_ref, weight_ref, positive_ref, ids_ref, gq_ref, gt_ref, gh_ref,
    xa, qq, qp, tz, ty, meta, info, s_in, s_hd, g_in, g_hd, st_in, st_hd, stat, wide, alpha,
    zs, zr, zown, cs, cr, yown, ys, yr, acc, ar, br, qown,
    h2, xap, qqp, h1s, h1r, hm, h2s, h2r, hzs, hzr,
    send_sem, recv_sem,
):
    rows, feat = qe_ref.shape
    half = rows // 2
    scale = feat ** -0.5
    cols = NZ * rows
    fhalf, fq = feat // 2, feat // 4
    blk, grp = lax.axis_index("blk"), lax.axis_index("group")
    xh, z = lax.div(blk, NZ), lax.rem(blk, NZ)
    xl, y, c = lax.div(grp, 2 * NY), lax.rem(lax.div(grp, 2), NY), lax.rem(grp, 2)

    def at(dz=0, dy=0, dx=0, dc=0):
        xh2 = 1 - xh if dx & 2 else xh
        xl2 = 1 - xl if dx & 1 else xl
        c2 = 1 - c if dc else c
        z2, y2 = lax.rem(z + dz + NZ, NZ), lax.rem(y + dy + NY, NY)
        return (xh2 * NZ + z2, (xl2 * NY + y2) * 2 + c2)

    def copy(src, dst, sem, device):
        return pltpu.make_async_remote_copy(
            src_ref=src, dst_ref=dst, send_sem=send_sem.at[sem], recv_sem=recv_sem.at[sem],
            device_id=device, device_id_type=MESH,
        )

    peers = (
        [at(dz=d) for d in (1, -1)] + [at(dy=d) for d in (1, -1)]
        + [at(dx=d) for d in (1, 2, 3)] + [at(dc=1)]
    )
    barrier = pltpu.get_barrier_semaphore()
    for peer in peers:
        pl.semaphore_signal(barrier, inc=1, device_id=peer, device_id_type=MESH)

    meta[1, 0:1, :] = weight_ref[...]
    meta[1, 1:2, :] = positive_ref[...].astype(F32)
    meta[1, 2:6, :] = ids_ref[...].astype(F32)
    meta[1, 6:8, :] = jnp.zeros((2, rows), F32)
    pl.semaphore_wait(barrier, len(peers))

    started = []

    def start(*args):
        one = copy(*args)
        one.start()
        started.append(one)
        return one

    zright, zleft = at(dz=1), at(dz=-1)
    yright, yleft = at(dy=1), at(dy=-1)
    core = at(dc=1)
    lo, hi = pl.ds(0, half), pl.ds(half, half)

    za, zb = {}, {}

    def gather_a(k):
        src = (te_ref.at[lo], te_ref.at[hi]) if k == 0 else (tz.at[NZ - k, lo], tz.at[k, hi])
        za[k] = (
            start(src[0], tz.at[NZ - 1 - k, lo], Z_AG + 2 * k, zright),
            start(src[1], tz.at[1 + k, hi], Z_AG + 2 * k + 1, zleft),
        )

    def gather_b(k):
        src = (te_ref.at[hi], te_ref.at[lo]) if k == 0 else (tz.at[NZ - k, hi], tz.at[k, lo])
        zb[k] = (
            start(src[0], tz.at[NZ - 1 - k, hi], Z_AG + 8 + 2 * k, zright),
            start(src[1], tz.at[1 + k, lo], Z_AG + 9 + 2 * k, zleft),
        )

    def arrive(pair):
        pair[0].wait_recv()
        pair[1].wait_recv()

    gather_a(0)
    m2 = start(meta.at[1], meta.at[2], X_IN + 3, at(dx=2))
    m1 = start(meta.at[1], meta.at[0], X_IN + 2, at(dx=1))
    x2 = start(qe_ref, xa.at[pl.ds(2 * rows, rows)], X_IN + 1, at(dx=2))
    x1 = start(qe_ref, xa.at[pl.ds(0, rows)], X_IN + 0, at(dx=1))
    yag = (
        start(te_ref, ty.at[3], Y_AG + 0, yright),
        start(te_ref, ty.at[1], Y_AG + 1, yleft),
    )
    gather_b(0)
    cag = [start(te_ref, ty.at[4], C_AG + 0, core)]

    tz[0] = te_ref[...]
    ty[0] = te_ref[...]
    xa[pl.ds(rows, rows), :] = qe_ref[...]

    def project(parts):
        def one(i):
            block = span(i, 256)
            left = jnp.concatenate([xa[pl.ds(p * rows, rows), :] for p in parts], axis=0)
            out = nn(left, head_ref[:, block]).astype(BF16)
            for n, p in enumerate(parts):
                qq[lax.div(i, 2), pl.ds((3 + p) * rows, rows), span(lax.rem(i, 2), 256)] = (
                    out[n * rows:(n + 1) * rows]
                )

        loop(feat // 256)(one)

    def project_back(parts):
        def one(i):
            block = span(i, 256)
            total = 0.0
            for h in range(2):
                left = jnp.concatenate(
                    [qq[h, pl.ds((3 + p) * rows, rows), :] for p in parts], axis=0
                )
                total += nt(left, head_ref[block, pl.ds(h * fhalf, fhalf)])
            out = (scale * total).astype(BF16)
            for n, p in enumerate(parts):
                qp[pl.ds(p * rows, rows), block] = out[n * rows:(n + 1) * rows]

        loop(feat // 256)(one)

    low, high, top_rows = pl.ds(0, rows), pl.ds(rows, rows), pl.ds(2 * rows, rows)

    def score_in(slot, where, what):
        s_in[where, pl.ds(slot * rows, rows)] = nt(qp[what, :], tz[slot])

    project([1])
    project_back([1])
    m1.wait_recv()
    m2.wait_recv()
    for p in range(3):
        wide[pl.ds(0, 8), :] = meta[p]
        info[pl.ds(p * rows, rows), :] = jnp.transpose(wide[...])

    lane = lax.broadcasted_iota(jnp.int32, (1, cols), 1)
    slot_of, row_of = lane // rows, lane % rows
    other = slot_of // NY
    owner_core = c + other - 2 * c * other
    owner = (xl * NY + lax.rem(y + slot_of % NY, NY)) * 2 + owner_core
    hard_col = (owner * (2 * cols) + blk * rows + row_of).astype(F32)
    in_col = (xh * cols + lax.rem(z * rows + lane, cols)).astype(F32)

    def mask_hard(i):
        block = span(i, 32)
        named = info[block, :]
        count = jnp.zeros((32, cols), F32)
        for k in range(4):
            count += jnp.where(named[:, 2 + k:3 + k] == hard_col, 1.0, 0.0)
        s_hd[block, :] = jnp.where(count > 0.0, jnp.log(jnp.maximum(count, 1.0)), NEG)

    def score_hard(where, slot):
        block = pl.ds(slot * rows, rows) if isinstance(slot, int) else span(slot, rows)
        s_hd[where, block] = s_hd[where, block] + nt(qp[where, :], ty[slot])

    arrive(za[0])
    gather_a(1)
    loop(rows // 32)(mask_hard)
    arrive(zb[0])
    gather_b(1)
    arrive(yag)
    yag2 = (
        start(ty.at[3, lo], ty.at[2, lo], Y_AG + 2, yright),
        start(ty.at[1, hi], ty.at[2, hi], Y_AG + 3, yleft),
    )
    cag.append(start(ty.at[3], ty.at[7], C_AG + 1, core))
    cag.append(start(ty.at[1], ty.at[5], C_AG + 2, core))
    loop(rows // 32)(lambda i: mask_hard(i + rows // 32))
    for slot in (0, 3, 1):
        score_hard(high, slot)
    arrive(za[1])
    gather_a(2)
    arrive(yag2)
    cag.append(start(ty.at[2], ty.at[6], C_AG + 3, core))
    arrive(zb[1])
    gather_b(2)

    def two_lanes(first, second):
        place = lax.broadcasted_iota(jnp.int32, (first.shape[0], 128), 1)
        return jnp.where(place == 0, first, second)

    def stats_hard(i):
        block = span(i, 32)
        kept = s_hd[block, :]
        top = jnp.max(kept, axis=1, keepdims=True)
        prob = jnp.exp(kept - top)
        s_hd[block, :] = prob
        st_hd[block, :] = two_lanes(top, jnp.sum(prob, axis=1, keepdims=True))

    x1.wait_recv()
    x2.wait_recv()
    early, late = pl.ds(0, 3 * rows), pl.ds(3 * rows, 3 * rows)
    operands = [start(xa.at[early], xap.at[early], H_IN + 0, core)]
    project([0, 2])
    operands.append(start(qq.at[1 - c, late], qqp.at[late], H_IN + 1, core))
    arrive(za[2])
    gather_a(3)
    project_back([0, 2])
    for one in cag:
        one.wait_recv()
    loop(2 * NY)(functools.partial(score_hard, low))
    for slot in (2, 4, 5, 6, 7):
        score_hard(high, slot)
    loop(2 * rows // 32)(stats_hard)
    for slot in (0, 7, 1, 6, 2):
        score_in(slot, pl.ds(0, 2 * rows), pl.ds(rows, 2 * rows))
    arrive(zb[2])
    for slot in (5, 3):
        score_in(slot, pl.ds(0, 2 * rows), pl.ds(rows, 2 * rows))

    left, right = pl.ds(0, 4 * rows), pl.ds(5 * rows, 3 * rows)
    last_cols = pl.ds(4 * rows, rows)

    def stats_most(i):
        block = span(i, 32)
        one, two = s_in[block, left], s_in[block, right]
        top = jnp.maximum(
            jnp.max(one, axis=1, keepdims=True), jnp.max(two, axis=1, keepdims=True)
        )
        one, two = jnp.exp(one - top), jnp.exp(two - top)
        s_in[block, left] = one
        s_in[block, right] = two
        total = jnp.sum(one, axis=1, keepdims=True) + jnp.sum(two, axis=1, keepdims=True)
        st_in[block, pl.ds(0, 128)] = two_lanes(top, total)

    loop(2 * rows // 32)(stats_most)
    arrive(za[3])
    score_in(4, pl.ds(0, 2 * rows), pl.ds(rows, 2 * rows))
    scores = s_in[:, last_cols]
    top = jnp.max(scores, axis=1, keepdims=True)
    prob = jnp.exp(scores - top)
    s_in[:, last_cols] = prob
    st_in[:, pl.ds(128, 128)] = two_lanes(top, jnp.sum(prob, axis=1, keepdims=True))

    place = lax.broadcasted_iota(jnp.int32, (rows, 128), 1)
    own, partner = pl.ds(0, rows), pl.ds(rows, rows)
    packed = jnp.zeros((rows, 128), F32)
    for where, value in enumerate((
        st_in[own, 0:1], st_in[own, 1:2], st_in[own, 128:129], st_in[own, 129:130],
        st_in[partner, 0:1], st_in[partner, 1:2], st_in[partner, 128:129], st_in[partner, 129:130],
        st_hd[partner, 0:1], st_hd[partner, 1:2], st_hd[own, 0:1], st_hd[own, 1:2],
    )):
        packed = jnp.where(place == where, value, packed)
    wide[...] = jnp.transpose(packed)

    def merge(parts):
        top = functools.reduce(jnp.maximum, [m for m, _ in parts])
        return top, sum(t * jnp.exp(m - top) for m, t in parts)

    def pair(ref, n):
        return ref[2 * n:2 * n + 1, :], ref[2 * n + 1:2 * n + 2, :]

    mine = merge([pair(wide, 0), pair(wide, 1), pair(wide, 4)])
    theirs = merge([pair(wide, 2), pair(wide, 3)])
    stat[0, 0:1, :], stat[0, 1:2, :] = mine
    stat[0, 2:3, :], stat[0, 3:4, :] = theirs
    stat[0, 4:6, :] = wide[10:12, :]
    stat[0, 6:8, :] = jnp.zeros((2, rows), F32)
    shared = [start(stat.at[0], stat.at[d], STAT + d - 1, at(dx=d)) for d in (1, 2, 3)]
    for one in shared:
        one.wait_recv()

    def log_total(parts):
        top, total = merge([pair(stat.at[d], n) for d, n in parts])
        return top + jnp.log(total)

    lse = [
        log_total([(0, 2), (1, 0), (3, 1)]),
        log_total([(0, 0), (1, 2), (2, 1)]),
        log_total([(0, 1), (2, 0), (3, 2)]),
    ]

    def factor(p, row):
        return meta[p, 0:1, :] * jnp.exp(wide[row:row + 1, :] - lse[p])

    factors = [
        factor(1, 0), factor(1, 2), factor(2, 4), factor(2, 6), factor(1, 8), factor(0, 10),
    ]
    for n, value in enumerate(factors):
        wide[n:n + 1, :] = value
    alpha[...] = jnp.transpose(wide[...])

    def grad_last(n):
        block = pl.ds(n * rows, rows)
        facts = info[pl.ds((1 + n) * rows, rows), :]
        hot = jnp.where(facts[:, 1:2] == in_col[:, 4 * rows:5 * rows], facts[:, 0:1], 0.0)
        a = alpha[:, 2 * n + 1:2 * n + 2]
        g_in[block, last_cols] = (a * s_in[block, last_cols] - hot).astype(BF16)

    grad_last(0)
    grad_last(1)

    def table_in(slot):
        return tn(g_in[:, pl.ds(slot * rows, rows)], qp[pl.ds(rows, 2 * rows), :])

    def table_pair(slot):
        both = tn(g_in[:, pl.ds(slot * rows, 2 * rows)], qp[pl.ds(rows, 2 * rows), :])
        zown[slot] = both[:rows]
        zown[slot + 1] = both[rows:]

    first = table_in(4).astype(BF16)
    zs[0, lo] = first[:half]
    zs[4, hi] = first[half:]
    ra, rb = {}, {}

    def reduce_a(k):
        ra[k] = (
            start(zs.at[k, lo], zr.at[k, lo], Z_RS + 2 * k, zright),
            start(zs.at[4 + k, hi], zr.at[4 + k, hi], Z_RS + 2 * k + 1, zleft),
        )

    def reduce_b(k):
        rb[k] = (
            start(zs.at[k, hi], zr.at[k, hi], Z_RS + 6 + 2 * k, zright),
            start(zs.at[4 + k, lo], zr.at[4 + k, lo], Z_RS + 7 + 2 * k, zleft),
        )

    def sum_a(k):
        arrive(ra[k])
        zs[k + 1, lo] = (zown[3 - k, lo] + zr[k, lo].astype(F32)).astype(BF16)
        zs[5 + k, hi] = (zown[5 + k, hi] + zr[4 + k, hi].astype(F32)).astype(BF16)
        reduce_a(k + 1)

    def sum_b(k):
        arrive(rb[k])
        zs[k + 1, hi] = (zown[3 - k, hi] + zr[k, hi].astype(F32)).astype(BF16)
        zs[5 + k, lo] = (zown[5 + k, lo] + zr[4 + k, lo].astype(F32)).astype(BF16)
        reduce_b(k + 1)

    reduce_a(0)

    def grad_most(n):
        def one(i):
            block = span(i, 32)
            place = pl.ds(pl.multiple_of(n * rows + i * 32, 32), 32)
            facts = info[pl.ds(pl.multiple_of((1 + n) * rows + i * 32, 32), 32), :]
            a, w, target = alpha[block, 2 * n:2 * n + 1], facts[:, 0:1], facts[:, 1:2]
            for part, begin, size in ((left, 0, 4 * rows), (right, 5 * rows, 3 * rows)):
                hot = jnp.where(target == in_col[:, begin:begin + size], w, 0.0)
                g_in[place, part] = (a * s_in[place, part] - hot).astype(BF16)

        loop(rows // 32)(one)

    grad_most(0)
    grad_most(1)

    def grad_hard(i):
        block = span(i, 32)
        g_hd[block, :] = (alpha[block, 5:6] * s_hd[block, :]).astype(BF16)
        place = pl.ds(pl.multiple_of(rows + i * 32, 32), 32)
        g_hd[place, :] = (alpha[block, 4:5] * s_hd[place, :]).astype(BF16)

    loop(rows // 32)(grad_hard)

    def table_hard(first):
        many = tn(g_hd[:, pl.ds(first * rows, NY * rows)], qp[pl.ds(0, 2 * rows), :])
        return many.reshape(NY, rows, feat)

    cs[...] = table_hard(NY).astype(BF16)
    cross = start(cs, cr, C_RS, core)

    table_pair(2)
    table_pair(5)
    zs[1, hi] = zown[3, hi].astype(BF16)
    zs[5, lo] = zown[5, lo].astype(BF16)
    reduce_b(1)

    def ahead(i):
        block = span(i, 256)
        a_in, a_hd = jnp.zeros((2 * rows, 256), F32), jnp.zeros((2 * rows, 256), F32)
        for n in range(NZ // 2):
            part, two = pl.ds(2 * n * rows, 2 * rows), pl.ds(2 * n, 2)
            a_in += nn(g_in[:, part], tz[two, :, block].reshape(2 * rows, 256))
            a_hd += nn(g_hd[:, part], ty[two, :, block].reshape(2 * rows, 256))
        at0 = 3 * rows
        xa[pl.ds(at0, rows), block] = (scale * a_hd[:rows]).astype(BF16)
        own_part = scale * (a_hd[rows:] + a_in[:rows])
        acc[:, block] = own_part
        xa[pl.ds(at0 + rows, rows), block] = own_part.astype(BF16)
        xa[pl.ds(at0 + 2 * rows, rows), block] = (scale * a_in[rows:]).astype(BF16)

    loop(feat // 256)(ahead)
    back1 = start(xa.at[pl.ds(3 * rows, rows)], ar.at[0], X_OUT + 0, at(dx=1))
    operands.append(start(xa.at[late], xap.at[late], H_IN + 2, core))
    cross.wait_recv()
    yown[...] = table_hard(0) + cr[...].astype(F32)
    ys[0, lo] = yown[2, lo].astype(BF16)
    ys[1, hi] = yown[2, hi].astype(BF16)
    yrs = (
        start(ys.at[0, lo], yr.at[0, lo], Y_RS + 0, yright),
        start(ys.at[1, hi], yr.at[1, hi], Y_RS + 1, yleft),
    )

    def through(i):
        part = nn(xa[pl.ds(3 * rows, 3 * rows), :], head_ref[:, span(i, 256)])
        qq[lax.div(i, 2), pl.ds(0, 3 * rows), span(lax.rem(i, 2), 256)] = part.astype(BF16)

    loop(feat // 256)(through)
    operands.append(start(qq.at[1 - c, early], qqp.at[early], H_IN + 3, core))
    sum_a(0)
    sum_b(1)
    zown[7] = table_in(7)
    table_pair(0)
    for one in operands:
        one.wait_recv()

    def head_part(i):
        block = span(i, 256)
        h2[block, :] = tn(xa[:, block], qq[c]) + tn(xap[:, block], qqp[...])

    loop(feat // 256)(head_part)

    groups = feat // (8 * NY)
    view_a = h2.reshape(groups, NY, 8, fhalf)
    view_b = h2.reshape(2, NZ, 2, 8 * NY, fhalf)

    def cross_x(d):
        return (1 - xh if d & 2 else xh), (1 - xl if d & 1 else xl)

    stage1 = []
    for d in (1, 2, 3):
        there = lax.rem(y + d, NY)
        h1s[d - 1] = view_a[:, there, :, 0:fq].reshape(groups * 8, fq).astype(BF16)
        stage1.append(start(h1s.at[d - 1], h1r.at[d - 1], H_A1 + d - 1, at(dy=d)))
        xh2, xl2 = cross_x(d)
        h1s[d + 2] = view_b[xh2, :, xl2, :, fq:fhalf].reshape(groups * 8, fq).astype(BF16)
        stage1.append(start(h1s.at[d + 2], h1r.at[d + 2], H_B1 + d - 1, at(dx=d)))
    sum_a(1)
    sum_b(2)

    hm[0] = view_a[:, y, :, 0:fq].reshape(groups * 8, fq)
    hm[1] = view_b[xh, :, xl, :, fq:fhalf].reshape(groups * 8, fq)
    sum_a(2)
    back1.wait_recv()
    ar[0] = (acc[...] + ar[0].astype(F32)).astype(BF16)

    def question_in(i):
        block = span(i, 256)
        qown[:, block] = nn(ar[0], head_ref[:, block])

    loop(feat // 256)(question_in)
    for one in stage1:
        one.wait_recv()
    for n in range(2):
        hm[n] = (hm[n] + h1r[3 * n].astype(F32)) + (
            h1r[3 * n + 1].astype(F32) + h1r[3 * n + 2].astype(F32)
        )
    part_a = hm.at[0].reshape(2, NZ, 2, 8, fq)
    part_b = hm.at[1].reshape(NZ, NY, 8, fq)
    stage2 = []
    for d in (1, 2, 3):
        xh2, xl2 = cross_x(d)
        h2s[d - 1] = part_a[xh2, :, xl2].reshape(NZ * 8, fq).astype(BF16)
        stage2.append(start(h2s.at[d - 1], h2r.at[d - 1], H_A2 + d - 1, at(dx=d)))
        there = lax.rem(y + d, NY)
        h2s[d + 2] = part_b[:, there].reshape(NZ * 8, fq).astype(BF16)
        stage2.append(start(h2s.at[d + 2], h2r.at[d + 2], H_B2 + d - 1, at(dy=d)))
    back2 = start(qq.at[:, pl.ds(2 * rows, rows)], br, X_OUT + 1, at(dx=2))
    arrive(yrs)
    ys[2, lo] = (yown[1, lo] + yr[0, lo].astype(F32)).astype(BF16)
    ys[2, hi] = yown[1, hi].astype(BF16)
    ys[3, lo] = yown[3, lo].astype(BF16)
    ys[3, hi] = (yown[3, hi] + yr[1, hi].astype(F32)).astype(BF16)
    yrs2 = (
        start(ys.at[2], yr.at[2], Y_RS + 2, yright),
        start(ys.at[3], yr.at[3], Y_RS + 3, yleft),
    )
    for one in stage2:
        one.wait_recv()
    small_a = part_a[xh, :, xl].reshape(NZ * 8, fq)
    small_b = part_b[:, y].reshape(NZ * 8, fq)
    for d in range(3):
        small_a = small_a + h2r[d].astype(F32)
        small_b = small_b + h2r[d + 3].astype(F32)
    hzs[:, :, pl.ds(0, fq)] = small_a.reshape(NZ, 8, fq)
    hzs[:, :, pl.ds(fq, fq)] = small_b.reshape(NZ, 8, fq)
    hz = [start(hzs.at[z], hzr.at[1, NZ - 1], H_Z + 2 * NZ - 2, core)]
    for d in (4, 3, 5, 2, 6, 1, 7):
        there = hzs.at[lax.rem(z + d, NZ)]
        hz.append(start(there, hzr.at[0, d - 1], H_Z + d - 1, at(dz=d)))
        hz.append(start(there, hzr.at[1, d - 1], H_Z + NZ - 2 + d, at(dz=d, dc=1)))

    back2.wait_recv()
    for h in range(2):
        part = pl.ds(h * fhalf, fhalf)
        ar[1, :, part] = (qown[:, part] + br[h].astype(F32)).astype(BF16)

    def question(i):
        block = span(i, 256)
        gq_ref[:, block] = nt(ar[1], head_ref[block, :]).astype(BF16)

    loop(feat // 256)(question)

    arrive(rb[3])
    arrive(yrs2)
    zown[0] = (zown[0] + yown[0]) + (yr[2].astype(F32) + yr[3].astype(F32))
    arrive(ra[3])
    gt_ref[...] = (zown[0] + (zr[3].astype(F32) + zr[7].astype(F32))).astype(BF16)

    for one in hz:
        one.wait_recv()
    near, far = hzs[z], hzr[1, NZ - 1]
    for d in range(NZ - 1):
        near, far = near + hzr[0, d], far + hzr[1, d]
    near = jnp.where(c == 0, near[0:4], near[4:8])
    far = jnp.where(c == 0, far[0:4], far[4:8])
    gh_ref[:, pl.ds(0, fhalf)] = jnp.where(c == 0, near, far)
    gh_ref[:, pl.ds(fhalf, fhalf)] = jnp.where(c == 0, far, near)

    for one in started:
        one.wait_send()


def hand_over(*refs):
    for source, target in zip(refs[:3], refs[3:]):
        target[...] = source[...]


def body(q_embed, t_embed, head, positive, hard_ids, loss_weight):
    rows, feat = q_embed.shape[1:]
    cols, fhalf, fq = NZ * rows, feat // 2, feat // 4
    vmem = pl.BlockSpec(memory_space=pltpu.VMEM)
    shapes = [
        ((6 * rows, feat), BF16),
        ((2, 6 * rows, fhalf), BF16),
        ((3 * rows, feat), BF16),
        ((NZ, rows, feat), BF16),
        ((2 * NY, rows, feat), BF16),
        ((3, 8, rows), F32),
        ((3 * rows, 128), F32),
        ((2 * rows, cols), F32),
        ((2 * rows, cols), F32),
        ((2 * rows, cols), BF16),
        ((2 * rows, cols), BF16),
        ((2 * rows, 256), F32),
        ((2 * rows, 128), F32),
        ((4, 8, rows), F32),
        ((128, rows), F32),
        ((rows, 128), F32),
        ((8, rows, feat), BF16),
        ((8, rows, feat), BF16),
        ((8, rows, feat), F32),
        ((NY, rows, feat), BF16),
        ((NY, rows, feat), BF16),
        ((NY, rows, feat), F32),
        ((4, rows, feat), BF16),
        ((4, rows, feat), BF16),
        ((rows, feat), F32),
        ((2, rows, feat), BF16),
        ((2, rows, fhalf), BF16),
        ((rows, feat), F32),
        ((feat, fhalf), F32),
        ((6 * rows, feat), BF16),
        ((6 * rows, fhalf), BF16),
        ((6, feat // NY, fq), BF16),
        ((6, feat // NY, fq), BF16),
        ((2, feat // NY, fq), F32),
        ((6, NZ * 8, fq), BF16),
        ((6, NZ * 8, fq), BF16),
        ((NZ, 8, fhalf), F32),
        ((2, NZ, 8, fhalf), F32),
    ]
    outs = (
        jax.ShapeDtypeStruct((rows, feat), BF16),
        jax.ShapeDtypeStruct((rows, feat), BF16),
        jax.ShapeDtypeStruct((4, feat), F32),
    )
    results = pl.pallas_call(
        kernel,
        out_shape=outs,
        in_specs=[vmem] * 6,
        out_specs=(vmem, vmem, vmem),
        scratch_shapes=[pltpu.VMEM(s, t) for s, t in shapes] + [
            pltpu.SemaphoreType.DMA((COPIES,)),
            pltpu.SemaphoreType.DMA((COPIES,)),
        ],
        compiler_params=pltpu.CompilerParams(
            collective_id=0, has_side_effects=True, vmem_limit_bytes=56 * 1024 * 1024
        ),
    )(q_embed[0], t_embed[0], head, loss_weight, positive, hard_ids[0].T)
    grad_q, grad_t, grad_head = pl.pallas_call(
        hand_over,
        out_shape=outs,
        in_specs=[vmem] * 3,
        out_specs=(vmem, vmem, vmem),
    )(*results)
    return (grad_q[None], grad_t[None], grad_head)


def solution(mesh):
    in_specs = (
        P("group", "blk", None),
        P("group", "blk", None),
        P(),
        P("group", "blk"),
        P("group", "blk", None),
        P("group", "blk"),
    )
    out_specs = (P("group", "blk", None), P("group", "blk", None), P(("blk", "group"), None))
    return jax.shard_map(body, mesh=mesh, in_specs=in_specs, out_specs=out_specs, check_vma=False)
```

```python
import functools
import math

import jax
import jax.numpy as jnp
from jax import lax
from jax.experimental import pallas as pl
from jax.experimental.pallas import tpu as pltpu
from jax.sharding import PartitionSpec as P

MESH = pl.DeviceIdType.MESH
F32 = jnp.float32
BF16 = jnp.bfloat16

NZ = 8
NY = 4
NEG = -1e30


Z_AG, Y_AG, C_AG, X_IN, STAT = 0, 14, 18, 22, 26
Z_RS, C_RS, Y_RS, X_OUT = 29, 43, 47, 51
H_IN, H_A1, H_B1, H_A2, H_B2, H_Z = 53, 57, 60, 63, 66, 69
COPIES = 84


def nn(left, right):
    return lax.dot_general(left, right, (((1,), (0,)), ((), ())), preferred_element_type=F32)


def nt(left, right):
    return lax.dot_general(left, right, (((1,), (1,)), ((), ())), preferred_element_type=F32)


def tn(left, right):
    return lax.dot_general(left, right, (((0,), (0,)), ((), ())), preferred_element_type=F32)


def span(i, size):
    return pl.ds(pl.multiple_of(i * size, size), size)


def loop(count, unroll=1):
    def run(step):
        lax.fori_loop(0, count, lambda i, carry: (step(i), carry)[1], 0, unroll=unroll)
    return run


def kernel(
    qe_ref, te_ref, head_ref, weight_ref, positive_ref, ids_ref, gq_ref, gt_ref, gh_ref,
    xa, qq, qp, tz, ty, meta, info, s_in, s_hd, g_in, g_hd, st_in, st_hd, stat, wide, alpha,
    zs, zr, zown, cs, cr, yown, ys, yr, acc, ar, br, qown,
    h2, xap, qqp, h1s, h1r, hm, h2s, h2r, hzs, hzr,
    send_sem, recv_sem,
):
    rows, feat = qe_ref.shape
    half = rows // 2
    scale = feat ** -0.5
    cols = NZ * rows
    fhalf, fq = feat // 2, feat // 4
    blk, grp = lax.axis_index("blk"), lax.axis_index("group")
    xh, z = lax.div(blk, NZ), lax.rem(blk, NZ)
    xl, y, c = lax.div(grp, 2 * NY), lax.rem(lax.div(grp, 2), NY), lax.rem(grp, 2)

    def at(dz=0, dy=0, dx=0, dc=0):
        xh2 = 1 - xh if dx & 2 else xh
        xl2 = 1 - xl if dx & 1 else xl
        c2 = 1 - c if dc else c
        z2, y2 = lax.rem(z + dz + NZ, NZ), lax.rem(y + dy + NY, NY)
        return (xh2 * NZ + z2, (xl2 * NY + y2) * 2 + c2)

    def copy(src, dst, sem, device):
        return pltpu.make_async_remote_copy(
            src_ref=src, dst_ref=dst, send_sem=send_sem.at[sem], recv_sem=recv_sem.at[sem],
            device_id=device, device_id_type=MESH,
        )

    peers = (
        [at(dz=d) for d in (1, -1)] + [at(dy=d) for d in (1, -1)]
        + [at(dx=d) for d in (1, 2, 3)] + [at(dc=1)]
    )
    barrier = pltpu.get_barrier_semaphore()
    for peer in peers:
        pl.semaphore_signal(barrier, inc=1, device_id=peer, device_id_type=MESH)

    meta[1, 0:1, :] = weight_ref[...]
    meta[1, 1:2, :] = positive_ref[...].astype(F32)
    meta[1, 2:6, :] = ids_ref[...].astype(F32)
    meta[1, 6:8, :] = jnp.zeros((2, rows), F32)
    pl.semaphore_wait(barrier, len(peers))

    started = []

    def start(*args):
        one = copy(*args)
        one.start()
        started.append(one)
        return one

    zright, zleft = at(dz=1), at(dz=-1)
    yright, yleft = at(dy=1), at(dy=-1)
    core = at(dc=1)
    lo, hi = pl.ds(0, half), pl.ds(half, half)

    za, zb = {}, {}

    def gather_a(k):
        src = (te_ref.at[lo], te_ref.at[hi]) if k == 0 else (tz.at[NZ - k, lo], tz.at[k, hi])
        za[k] = (
            start(src[0], tz.at[NZ - 1 - k, lo], Z_AG + 2 * k, zright),
            start(src[1], tz.at[1 + k, hi], Z_AG + 2 * k + 1, zleft),
        )

    def gather_b(k):
        src = (te_ref.at[hi], te_ref.at[lo]) if k == 0 else (tz.at[NZ - k, hi], tz.at[k, lo])
        zb[k] = (
            start(src[0], tz.at[NZ - 1 - k, hi], Z_AG + 8 + 2 * k, zright),
            start(src[1], tz.at[1 + k, lo], Z_AG + 9 + 2 * k, zleft),
        )

    def arrive(pair):
        pair[0].wait_recv()
        pair[1].wait_recv()

    gather_a(0)
    m2 = start(meta.at[1], meta.at[2], X_IN + 3, at(dx=2))
    m1 = start(meta.at[1], meta.at[0], X_IN + 2, at(dx=1))
    x2 = start(qe_ref, xa.at[pl.ds(2 * rows, rows)], X_IN + 1, at(dx=2))
    x1 = start(qe_ref, xa.at[pl.ds(0, rows)], X_IN + 0, at(dx=1))
    yag = (
        start(te_ref, ty.at[3], Y_AG + 0, yright),
        start(te_ref, ty.at[1], Y_AG + 1, yleft),
    )
    gather_b(0)
    cag = [start(te_ref, ty.at[4], C_AG + 0, core)]

    tz[0] = te_ref[...]
    ty[0] = te_ref[...]
    xa[pl.ds(rows, rows), :] = qe_ref[...]

    def project(parts):
        def one(i):
            block = span(i, 256)
            left = jnp.concatenate([xa[pl.ds(p * rows, rows), :] for p in parts], axis=0)
            out = nn(left, head_ref[:, block]).astype(BF16)
            for n, p in enumerate(parts):
                qq[lax.div(i, 2), pl.ds((3 + p) * rows, rows), span(lax.rem(i, 2), 256)] = (
                    out[n * rows:(n + 1) * rows]
                )

        loop(feat // 256)(one)

    def project_back(parts):
        def one(i):
            block = span(i, 256)
            total = 0.0
            for h in range(2):
                left = jnp.concatenate(
                    [qq[h, pl.ds((3 + p) * rows, rows), :] for p in parts], axis=0
                )
                total += nt(left, head_ref[block, pl.ds(h * fhalf, fhalf)])
            out = (scale * total).astype(BF16)
            for n, p in enumerate(parts):
                qp[pl.ds(p * rows, rows), block] = out[n * rows:(n + 1) * rows]

        loop(feat // 256)(one)

    low, high, top_rows = pl.ds(0, rows), pl.ds(rows, rows), pl.ds(2 * rows, rows)

    def score_in(slot, where, what):
        s_in[where, pl.ds(slot * rows, rows)] = nt(qp[what, :], tz[slot])

    project([1])
    project_back([1])
    m1.wait_recv()
    m2.wait_recv()
    for p in range(3):
        wide[pl.ds(0, 8), :] = meta[p]
        info[pl.ds(p * rows, rows), :] = jnp.transpose(wide[...])

    lane = lax.broadcasted_iota(jnp.int32, (1, cols), 1)
    slot_of, row_of = lane // rows, lane % rows
    other = slot_of // NY
    owner_core = c + other - 2 * c * other
    owner = (xl * NY + lax.rem(y + slot_of % NY, NY)) * 2 + owner_core
    hard_col = (owner * (2 * cols) + blk * rows + row_of).astype(F32)
    in_col = (xh * cols + lax.rem(z * rows + lane, cols)).astype(F32)

    def mask_hard(i):
        block = span(i, 32)
        named = info[block, :]
        count = jnp.zeros((32, cols), F32)
        for k in range(4):
            count += jnp.where(named[:, 2 + k:3 + k] == hard_col, 1.0, 0.0)
        s_hd[block, :] = jnp.where(count > 0.0, jnp.log(jnp.maximum(count, 1.0)), NEG)

    def score_hard(where, slot):
        block = pl.ds(slot * rows, rows) if isinstance(slot, int) else span(slot, rows)
        s_hd[where, block] = s_hd[where, block] + nt(qp[where, :], ty[slot])

    arrive(za[0])
    gather_a(1)
    loop(rows // 32)(mask_hard)
    arrive(zb[0])
    gather_b(1)
    arrive(yag)
    yag2 = (
        start(ty.at[3, lo], ty.at[2, lo], Y_AG + 2, yright),
        start(ty.at[1, hi], ty.at[2, hi], Y_AG + 3, yleft),
    )
    cag.append(start(ty.at[3], ty.at[7], C_AG + 1, core))
    cag.append(start(ty.at[1], ty.at[5], C_AG + 2, core))
    loop(rows // 32)(lambda i: mask_hard(i + rows // 32))
    for slot in (0, 3, 1):
        score_hard(high, slot)
    arrive(za[1])
    gather_a(2)
    arrive(yag2)
    cag.append(start(ty.at[2], ty.at[6], C_AG + 3, core))
    arrive(zb[1])
    gather_b(2)

    def two_lanes(first, second):
        place = lax.broadcasted_iota(jnp.int32, (first.shape[0], 128), 1)
        return jnp.where(place == 0, first, second)

    def stats_hard(i):
        block = span(i, 32)
        kept = s_hd[block, :]
        top = jnp.max(kept, axis=1, keepdims=True)
        prob = jnp.exp(kept - top)
        s_hd[block, :] = prob
        st_hd[block, :] = two_lanes(top, jnp.sum(prob, axis=1, keepdims=True))

    x1.wait_recv()
    x2.wait_recv()
    early, late = pl.ds(0, 3 * rows), pl.ds(3 * rows, 3 * rows)
    operands = [start(xa.at[early], xap.at[early], H_IN + 0, core)]
    project([0, 2])
    operands.append(start(qq.at[1 - c, late], qqp.at[late], H_IN + 1, core))
    arrive(za[2])
    gather_a(3)
    project_back([0, 2])
    for one in cag:
        one.wait_recv()
    loop(2 * NY)(functools.partial(score_hard, low))
    for slot in (2, 4, 5, 6, 7):
        score_hard(high, slot)
    loop(2 * rows // 32)(stats_hard)
    for slot in (0, 7, 1, 6, 2):
        score_in(slot, pl.ds(0, 2 * rows), pl.ds(rows, 2 * rows))
    arrive(zb[2])
    for slot in (5, 3):
        score_in(slot, pl.ds(0, 2 * rows), pl.ds(rows, 2 * rows))

    left, right = pl.ds(0, 4 * rows), pl.ds(5 * rows, 3 * rows)
    last_cols = pl.ds(4 * rows, rows)

    def stats_most(i):
        block = span(i, 32)
        one, two = s_in[block, left], s_in[block, right]
        top = jnp.maximum(
            jnp.max(one, axis=1, keepdims=True), jnp.max(two, axis=1, keepdims=True)
        )
        one, two = jnp.exp(one - top), jnp.exp(two - top)
        s_in[block, left] = one
        s_in[block, right] = two
        total = jnp.sum(one, axis=1, keepdims=True) + jnp.sum(two, axis=1, keepdims=True)
        st_in[block, pl.ds(0, 128)] = two_lanes(top, total)

    loop(2 * rows // 32)(stats_most)
    arrive(za[3])
    score_in(4, pl.ds(0, 2 * rows), pl.ds(rows, 2 * rows))
    scores = s_in[:, last_cols]
    top = jnp.max(scores, axis=1, keepdims=True)
    prob = jnp.exp(scores - top)
    s_in[:, last_cols] = prob
    st_in[:, pl.ds(128, 128)] = two_lanes(top, jnp.sum(prob, axis=1, keepdims=True))

    place = lax.broadcasted_iota(jnp.int32, (rows, 128), 1)
    own, partner = pl.ds(0, rows), pl.ds(rows, rows)
    packed = jnp.zeros((rows, 128), F32)
    for where, value in enumerate((
        st_in[own, 0:1], st_in[own, 1:2], st_in[own, 128:129], st_in[own, 129:130],
        st_in[partner, 0:1], st_in[partner, 1:2], st_in[partner, 128:129], st_in[partner, 129:130],
        st_hd[partner, 0:1], st_hd[partner, 1:2], st_hd[own, 0:1], st_hd[own, 1:2],
    )):
        packed = jnp.where(place == where, value, packed)
    wide[...] = jnp.transpose(packed)

    def merge(parts):
        top = functools.reduce(jnp.maximum, [m for m, _ in parts])
        return top, sum(t * jnp.exp(m - top) for m, t in parts)

    def pair(ref, n):
        return ref[2 * n:2 * n + 1, :], ref[2 * n + 1:2 * n + 2, :]

    mine = merge([pair(wide, 0), pair(wide, 1), pair(wide, 4)])
    theirs = merge([pair(wide, 2), pair(wide, 3)])
    stat[0, 0:1, :], stat[0, 1:2, :] = mine
    stat[0, 2:3, :], stat[0, 3:4, :] = theirs
    stat[0, 4:6, :] = wide[10:12, :]
    stat[0, 6:8, :] = jnp.zeros((2, rows), F32)
    shared = [start(stat.at[0], stat.at[d], STAT + d - 1, at(dx=d)) for d in (2, 1, 3)]
    for one in shared:
        one.wait_recv()

    def log_total(parts):
        top, total = merge([pair(stat.at[d], n) for d, n in parts])
        return top + jnp.log(total)

    lse = [
        log_total([(0, 2), (1, 0), (3, 1)]),
        log_total([(0, 0), (1, 2), (2, 1)]),
        log_total([(0, 1), (2, 0), (3, 2)]),
    ]

    def factor(p, row):
        return meta[p, 0:1, :] * jnp.exp(wide[row:row + 1, :] - lse[p])

    factors = [
        factor(1, 0), factor(1, 2), factor(2, 4), factor(2, 6), factor(1, 8), factor(0, 10),
    ]
    for n, value in enumerate(factors):
        wide[n:n + 1, :] = value
    alpha[...] = jnp.transpose(wide[...])

    def grad_last(n):
        block = pl.ds(n * rows, rows)
        facts = info[pl.ds((1 + n) * rows, rows), :]
        hot = jnp.where(facts[:, 1:2] == in_col[:, 4 * rows:5 * rows], facts[:, 0:1], 0.0)
        a = alpha[:, 2 * n + 1:2 * n + 2]
        g_in[block, last_cols] = (a * s_in[block, last_cols] - hot).astype(BF16)

    grad_last(0)
    grad_last(1)

    def table_in(slot):
        return tn(g_in[:, pl.ds(slot * rows, rows)], qp[pl.ds(rows, 2 * rows), :])

    def table_pair(slot):
        both = tn(g_in[:, pl.ds(slot * rows, 2 * rows)], qp[pl.ds(rows, 2 * rows), :])
        zown[slot] = both[:rows]
        zown[slot + 1] = both[rows:]

    first = table_in(4).astype(BF16)
    zs[0, lo] = first[:half]
    zs[4, hi] = first[half:]
    ra, rb = {}, {}

    def reduce_a(k):
        ra[k] = (
            start(zs.at[k, lo], zr.at[k, lo], Z_RS + 2 * k, zright),
            start(zs.at[4 + k, hi], zr.at[4 + k, hi], Z_RS + 2 * k + 1, zleft),
        )

    def reduce_b(k):
        rb[k] = (
            start(zs.at[k, hi], zr.at[k, hi], Z_RS + 6 + 2 * k, zright),
            start(zs.at[4 + k, lo], zr.at[4 + k, lo], Z_RS + 7 + 2 * k, zleft),
        )

    def sum_a(k):
        arrive(ra[k])
        zs[k + 1, lo] = (zown[3 - k, lo] + zr[k, lo].astype(F32)).astype(BF16)
        zs[5 + k, hi] = (zown[5 + k, hi] + zr[4 + k, hi].astype(F32)).astype(BF16)
        reduce_a(k + 1)

    def sum_b(k):
        arrive(rb[k])
        zs[k + 1, hi] = (zown[3 - k, hi] + zr[k, hi].astype(F32)).astype(BF16)
        zs[5 + k, lo] = (zown[5 + k, lo] + zr[4 + k, lo].astype(F32)).astype(BF16)
        reduce_b(k + 1)

    reduce_a(0)

    def grad_most(n):
        def one(i):
            block = span(i, 32)
            place = pl.ds(pl.multiple_of(n * rows + i * 32, 32), 32)
            facts = info[pl.ds(pl.multiple_of((1 + n) * rows + i * 32, 32), 32), :]
            a, w, target = alpha[block, 2 * n:2 * n + 1], facts[:, 0:1], facts[:, 1:2]
            for part, begin, size in ((left, 0, 4 * rows), (right, 5 * rows, 3 * rows)):
                hot = jnp.where(target == in_col[:, begin:begin + size], w, 0.0)
                g_in[place, part] = (a * s_in[place, part] - hot).astype(BF16)

        loop(rows // 32)(one)

    grad_most(0)
    grad_most(1)

    def grad_hard(i):
        block = span(i, 32)
        g_hd[block, :] = (alpha[block, 5:6] * s_hd[block, :]).astype(BF16)
        place = pl.ds(pl.multiple_of(rows + i * 32, 32), 32)
        g_hd[place, :] = (alpha[block, 4:5] * s_hd[place, :]).astype(BF16)

    loop(rows // 32)(grad_hard)

    def table_hard(first):
        many = tn(g_hd[:, pl.ds(first * rows, NY * rows)], qp[pl.ds(0, 2 * rows), :])
        return many.reshape(NY, rows, feat)

    cs[...] = table_hard(NY).astype(BF16)
    cross = start(cs, cr, C_RS, core)

    table_pair(2)
    table_pair(5)
    zs[1, hi] = zown[3, hi].astype(BF16)
    zs[5, lo] = zown[5, lo].astype(BF16)
    reduce_b(1)

    def ahead(i):
        block = span(i, 256)
        a_in, a_hd = jnp.zeros((2 * rows, 256), F32), jnp.zeros((2 * rows, 256), F32)
        for n in range(NZ // 2):
            part, two = pl.ds(2 * n * rows, 2 * rows), pl.ds(2 * n, 2)
            a_in += nn(g_in[:, part], tz[two, :, block].reshape(2 * rows, 256))
            a_hd += nn(g_hd[:, part], ty[two, :, block].reshape(2 * rows, 256))
        at0 = 3 * rows
        xa[pl.ds(at0, rows), block] = (scale * a_hd[:rows]).astype(BF16)
        own_part = scale * (a_hd[rows:] + a_in[:rows])
        acc[:, block] = own_part
        xa[pl.ds(at0 + rows, rows), block] = own_part.astype(BF16)
        xa[pl.ds(at0 + 2 * rows, rows), block] = (scale * a_in[rows:]).astype(BF16)

    loop(feat // 256)(ahead)
    back1 = start(xa.at[pl.ds(3 * rows, rows)], ar.at[0], X_OUT + 0, at(dx=1))
    operands.append(start(xa.at[late], xap.at[late], H_IN + 2, core))
    cross.wait_recv()
    yown[...] = table_hard(0) + cr[...].astype(F32)
    ys[0, lo] = yown[2, lo].astype(BF16)
    ys[1, hi] = yown[2, hi].astype(BF16)
    yrs = (
        start(ys.at[0, lo], yr.at[0, lo], Y_RS + 0, yright),
        start(ys.at[1, hi], yr.at[1, hi], Y_RS + 1, yleft),
    )

    def through(i):
        part = nn(xa[pl.ds(3 * rows, 3 * rows), :], head_ref[:, span(i, 256)])
        qq[lax.div(i, 2), pl.ds(0, 3 * rows), span(lax.rem(i, 2), 256)] = part.astype(BF16)

    loop(feat // 256)(through)
    operands.append(start(qq.at[1 - c, early], qqp.at[early], H_IN + 3, core))
    sum_a(0)
    sum_b(1)
    zown[7] = table_in(7)
    table_pair(0)
    for one in operands:
        one.wait_recv()

    def head_part(i):
        block = span(i, 256)
        h2[block, :] = tn(xa[:, block], qq[c]) + tn(xap[:, block], qqp[...])

    loop(feat // 256)(head_part)

    groups = feat // (8 * NY)
    view_a = h2.reshape(groups, NY, 8, fhalf)
    view_b = h2.reshape(2, NZ, 2, 8 * NY, fhalf)

    def cross_x(d):
        return (1 - xh if d & 2 else xh), (1 - xl if d & 1 else xl)

    stage1 = []
    for d in (2, 1, 3):
        there = lax.rem(y + d, NY)
        h1s[d - 1] = view_a[:, there, :, 0:fq].reshape(groups * 8, fq).astype(BF16)
        stage1.append(start(h1s.at[d - 1], h1r.at[d - 1], H_A1 + d - 1, at(dy=d)))
        xh2, xl2 = cross_x(d)
        h1s[d + 2] = view_b[xh2, :, xl2, :, fq:fhalf].reshape(groups * 8, fq).astype(BF16)
        stage1.append(start(h1s.at[d + 2], h1r.at[d + 2], H_B1 + d - 1, at(dx=d)))
    sum_a(1)
    sum_b(2)

    hm[0] = view_a[:, y, :, 0:fq].reshape(groups * 8, fq)
    hm[1] = view_b[xh, :, xl, :, fq:fhalf].reshape(groups * 8, fq)
    sum_a(2)
    back1.wait_recv()
    ar[0] = (acc[...] + ar[0].astype(F32)).astype(BF16)

    def question_in(i):
        block = span(i, 256)
        qown[:, block] = nn(ar[0], head_ref[:, block])

    loop(feat // 256)(question_in)
    for one in stage1:
        one.wait_recv()
    for n in range(2):
        hm[n] = (hm[n] + h1r[3 * n].astype(F32)) + (
            h1r[3 * n + 1].astype(F32) + h1r[3 * n + 2].astype(F32)
        )
    part_a = hm.at[0].reshape(2, NZ, 2, 8, fq)
    part_b = hm.at[1].reshape(NZ, NY, 8, fq)
    stage2 = []
    for d in (2, 1, 3):
        xh2, xl2 = cross_x(d)
        h2s[d - 1] = part_a[xh2, :, xl2].reshape(NZ * 8, fq).astype(BF16)
        stage2.append(start(h2s.at[d - 1], h2r.at[d - 1], H_A2 + d - 1, at(dx=d)))
        there = lax.rem(y + d, NY)
        h2s[d + 2] = part_b[:, there].reshape(NZ * 8, fq).astype(BF16)
        stage2.append(start(h2s.at[d + 2], h2r.at[d + 2], H_B2 + d - 1, at(dy=d)))
    back2 = start(qq.at[:, pl.ds(2 * rows, rows)], br, X_OUT + 1, at(dx=2))
    arrive(yrs)
    ys[2, lo] = (yown[1, lo] + yr[0, lo].astype(F32)).astype(BF16)
    ys[2, hi] = yown[1, hi].astype(BF16)
    ys[3, lo] = yown[3, lo].astype(BF16)
    ys[3, hi] = (yown[3, hi] + yr[1, hi].astype(F32)).astype(BF16)
    yrs2 = (
        start(ys.at[2], yr.at[2], Y_RS + 2, yright),
        start(ys.at[3], yr.at[3], Y_RS + 3, yleft),
    )
    for one in stage2:
        one.wait_recv()
    small_a = part_a[xh, :, xl].reshape(NZ * 8, fq)
    small_b = part_b[:, y].reshape(NZ * 8, fq)
    for d in range(3):
        small_a = small_a + h2r[d].astype(F32)
        small_b = small_b + h2r[d + 3].astype(F32)
    hzs[:, :, pl.ds(0, fq)] = small_a.reshape(NZ, 8, fq)
    hzs[:, :, pl.ds(fq, fq)] = small_b.reshape(NZ, 8, fq)
    hz = [start(hzs.at[z], hzr.at[1, NZ - 1], H_Z + 2 * NZ - 2, core)]
    for d in (4, 3, 5, 2, 6, 1, 7):
        there = hzs.at[lax.rem(z + d, NZ)]
        hz.append(start(there, hzr.at[0, d - 1], H_Z + d - 1, at(dz=d)))
        hz.append(start(there, hzr.at[1, d - 1], H_Z + NZ - 2 + d, at(dz=d, dc=1)))

    back2.wait_recv()
    for h in range(2):
        part = pl.ds(h * fhalf, fhalf)
        ar[1, :, part] = (qown[:, part] + br[h].astype(F32)).astype(BF16)

    def question(i):
        block = span(i, 256)
        gq_ref[:, block] = nt(ar[1], head_ref[block, :]).astype(BF16)

    loop(feat // 256)(question)

    arrive(rb[3])
    arrive(yrs2)
    zown[0] = (zown[0] + yown[0]) + (yr[2].astype(F32) + yr[3].astype(F32))
    arrive(ra[3])
    gt_ref[...] = (zown[0] + (zr[3].astype(F32) + zr[7].astype(F32))).astype(BF16)

    for one in hz:
        one.wait_recv()
    near, far = hzs[z], hzr[1, NZ - 1]
    for d in range(NZ - 1):
        near, far = near + hzr[0, d], far + hzr[1, d]
    near = jnp.where(c == 0, near[0:4], near[4:8])
    far = jnp.where(c == 0, far[0:4], far[4:8])
    gh_ref[:, pl.ds(0, fhalf)] = jnp.where(c == 0, near, far)
    gh_ref[:, pl.ds(fhalf, fhalf)] = jnp.where(c == 0, far, near)

    for one in started:
        one.wait_send()


def hand_over(*refs):
    for source, target in zip(refs[:3], refs[3:]):
        target[...] = source[...]


def body(q_embed, t_embed, head, positive, hard_ids, loss_weight):
    rows, feat = q_embed.shape[1:]
    cols, fhalf, fq = NZ * rows, feat // 2, feat // 4
    vmem = pl.BlockSpec(memory_space=pltpu.VMEM)
    shapes = [
        ((6 * rows, feat), BF16),
        ((2, 6 * rows, fhalf), BF16),
        ((3 * rows, feat), BF16),
        ((NZ, rows, feat), BF16),
        ((2 * NY, rows, feat), BF16),
        ((3, 8, rows), F32),
        ((3 * rows, 128), F32),
        ((2 * rows, cols), F32),
        ((2 * rows, cols), F32),
        ((2 * rows, cols), BF16),
        ((2 * rows, cols), BF16),
        ((2 * rows, 256), F32),
        ((2 * rows, 128), F32),
        ((4, 8, rows), F32),
        ((128, rows), F32),
        ((rows, 128), F32),
        ((8, rows, feat), BF16),
        ((8, rows, feat), BF16),
        ((8, rows, feat), F32),
        ((NY, rows, feat), BF16),
        ((NY, rows, feat), BF16),
        ((NY, rows, feat), F32),
        ((4, rows, feat), BF16),
        ((4, rows, feat), BF16),
        ((rows, feat), F32),
        ((2, rows, feat), BF16),
        ((2, rows, fhalf), BF16),
        ((rows, feat), F32),
        ((feat, fhalf), F32),
        ((6 * rows, feat), BF16),
        ((6 * rows, fhalf), BF16),
        ((6, feat // NY, fq), BF16),
        ((6, feat // NY, fq), BF16),
        ((2, feat // NY, fq), F32),
        ((6, NZ * 8, fq), BF16),
        ((6, NZ * 8, fq), BF16),
        ((NZ, 8, fhalf), F32),
        ((2, NZ, 8, fhalf), F32),
    ]
    outs = (
        jax.ShapeDtypeStruct((rows, feat), BF16),
        jax.ShapeDtypeStruct((rows, feat), BF16),
        jax.ShapeDtypeStruct((4, feat), F32),
    )
    results = pl.pallas_call(
        kernel,
        out_shape=outs,
        in_specs=[vmem] * 6,
        out_specs=(vmem, vmem, vmem),
        scratch_shapes=[pltpu.VMEM(s, t) for s, t in shapes] + [
            pltpu.SemaphoreType.DMA((COPIES,)),
            pltpu.SemaphoreType.DMA((COPIES,)),
        ],
        compiler_params=pltpu.CompilerParams(
            collective_id=0, has_side_effects=True, vmem_limit_bytes=56 * 1024 * 1024
        ),
    )(q_embed[0], t_embed[0], head, loss_weight, positive, hard_ids[0].T)
    grad_q, grad_t, grad_head = pl.pallas_call(
        hand_over,
        out_shape=outs,
        in_specs=[vmem] * 3,
        out_specs=(vmem, vmem, vmem),
    )(*results)
    return (grad_q[None], grad_t[None], grad_head)


def solution(mesh):
    in_specs = (
        P("group", "blk", None),
        P("group", "blk", None),
        P(),
        P("group", "blk"),
        P("group", "blk", None),
        P("group", "blk"),
    )
    out_specs = (P("group", "blk", None), P("group", "blk", None), P(("blk", "group"), None))
    return jax.shard_map(body, mesh=mesh, in_specs=in_specs, out_specs=out_specs, check_vma=False)
```
